32 devices in a mesh: seq: 16 (over z, y, core), dp: 2 (over x).
Axes of the slice: x: 2, y: 2, z: 4, core: 2. Of those that a mesh axis runs over, the one named last changes fastest.
Arguments:
- tokens: float32 [32, 256, 1152], P(('seq', 'dp')), may hold values from -6 to 6
- condition: float32 [32, 1152], P(('seq', 'dp')), may hold values from -8 to 8
- kept_tokens: int32 [32, 256], P(('seq', 'dp')), may hold values from 0 to 1, as said below
- grad_out: float32 [32, 256, 1152], P(('seq', 'dp')), may hold values from -6 to 6
- entry_weight: float32 [1152, 3456], P('seq', 'dp'), may hold values from -0.1875 to 0.1875
- merge_weight: float32 [1152, 1152], P('seq', 'dp'), may hold values from -1 to 1
- expand_weight: float32 [1152, 4608], P('seq', 'dp'), may hold values from -0.1875 to 0.1875
- shrink_weight: float32 [4608, 1152], P('seq', 'dp'), may hold values from -0.09375 to 0.09375
- modulate_weight: float32 [1152, 6912], P('seq', 'dp'), may hold values from -0.1875 to 0.1875
- entry_velocity: float32 [1152, 3456], P('seq', 'dp'), may hold values from -160 to 160
- merge_velocity: float32 [1152, 1152], P('seq', 'dp'), may hold values from -160 to 160
- expand_velocity: float32 [1152, 4608], P('seq', 'dp'), may hold values from -160 to 160
- shrink_velocity: float32 [4608, 1152], P('seq', 'dp'), may hold values from -160 to 160
- modulate_velocity: float32 [1152, 6912], P('seq', 'dp'), may hold values from -160 to 160
- entry_average: float32 [1152, 3456], P('seq', 'dp'), may hold values from -0.1875 to 0.1875
- merge_average: float32 [1152, 1152], P('seq', 'dp'), may hold values from -1 to 1
- expand_average: float32 [1152, 4608], P('seq', 'dp'), may hold values from -0.1875 to 0.1875
- shrink_average: float32 [4608, 1152], P('seq', 'dp'), may hold values from -0.09375 to 0.09375
- modulate_average: float32 [1152, 6912], P('seq', 'dp'), may hold values from -0.1875 to 0.1875
Outputs:
- output: float32 [32, 256, 1152], P(('seq', 'dp'))
- grad_tokens: float32 [32, 256, 1152], P(('seq', 'dp'))
- entry_next: float32 [1152, 3456], P('seq', 'dp')
- merge_next: float32 [1152, 1152], P('seq', 'dp')
- expand_next: float32 [1152, 4608], P('seq', 'dp')
- shrink_next: float32 [4608, 1152], P('seq', 'dp')
- modulate_next: float32 [1152, 6912], P('seq', 'dp')
- entry_velocity_next: float32 [1152, 3456], P('seq', 'dp')
- merge_velocity_next: float32 [1152, 1152], P('seq', 'dp')
- expand_velocity_next: float32 [1152, 4608], P('seq', 'dp')
- shrink_velocity_next: float32 [4608, 1152], P('seq', 'dp')
- modulate_velocity_next: float32 [1152, 6912], P('seq', 'dp')
- entry_average_next: float32 [1152, 3456], P('seq', 'dp')
- merge_average_next: float32 [1152, 1152], P('seq', 'dp')
- expand_average_next: float32 [1152, 4608], P('seq', 'dp')
- shrink_average_next: float32 [4608, 1152], P('seq', 'dp')
- modulate_average_next: float32 [1152, 6912], P('seq', 'dp')
The draws below stay inside these ranges and needn't reach their ends.
Inputs may be any that keep to these rules, and one draw needn't show every extreme that they name: `kept_tokens`: each latent keeps between 160 and 192 of its 256 slots, the number varying from latent to latent, the slots scattered at random.
All inputs are finite; a program needn't handle non-finite values.
Results may differ from the reference program's by a relative error of at most 0.02.
The reference program's roundings to bfloat16 on the way count: a program that leaves them out, or rounds other values in their place, can miss the bound.
Values may be sent and summed in bfloat16 or wider, within the bound.
No kernel may reach another device: no remote copies, remote signals or barrier semaphores. Data moves between devices by JAX's collectives and lax.ppermute only.
A program may use at most 192 MiB of HBM per device.

```python
import math
import jax
import jax.numpy as jnp
from jax import lax

D = 1152
HEADS = 16
FF = 4608
P_SIZE = 256
LATENTS = 32


def draw_kept_tokens(key, part):
    key = jax.random.fold_in(key, 7)
    count_key, order_key = jax.random.split(key)
    counts = jax.random.randint(count_key, (LATENTS, 1), P_SIZE * 5 // 8, P_SIZE * 3 // 4 + 1)
    orders = jax.vmap(lambda single: jax.random.permutation(single, P_SIZE))(jax.random.split(order_key, LATENTS))
    return (orders < counts).astype(jnp.int32)


def levels(key, extent, shards, smallest, high):
    level = 1.0
    for axis_at, shards_of in shards:
        draws = jax.random.uniform(jax.random.fold_in(jax.random.fold_in(key, 6), axis_at), (shards_of,), jnp.float32, smallest / len(shards), high / len(shards))
        level = level * jnp.repeat(jnp.exp(draws), extent[axis_at] // shards_of).reshape((-1,) + (1,) * (len(extent) - 1 - axis_at))
    return level


def bell_draw(rng, shape, deviation, limit, cuts=(), held_as=jnp.bfloat16):
    array = jax.random.normal(rng, shape, jnp.float32) * deviation
    if len(cuts) > 0:
        array = levels(rng, shape, cuts, -0.22, 0.18) * array
    return jnp.clip(array, min=-limit, max=limit).astype(held_as)


def setup_inputs(seed: int = 0) -> dict:
    streams_of = jax.random.split(jax.random.key(seed), 20)
    tokens = bell_draw(streams_of[0], (LATENTS, P_SIZE, D), 1.0, 6.0, ((0, 32),), jnp.float32)
    condition = bell_draw(streams_of[1], (LATENTS, D), 1.5, 8.0, ((0, 32),), jnp.float32)
    kept_tokens = draw_kept_tokens(jax.random.fold_in(streams_of[19], 71), 0)
    grad_out = bell_draw(streams_of[3], (LATENTS, P_SIZE, D), 1.0, 6.0, ((0, 32),), jnp.float32)
    entry_weight = bell_draw(streams_of[4], (D, 3 * D), D ** -0.5, 0.1875, ((0, 16), (1, 2)), jnp.float32)
    merge_weight = bell_draw(streams_of[5], (D, D), (D // 32) ** -0.5, 1.0, ((0, 16), (1, 2)), jnp.float32)
    expand_weight = bell_draw(streams_of[6], (D, FF), D ** -0.5, 0.1875, ((0, 16), (1, 2)), jnp.float32)
    shrink_weight = bell_draw(streams_of[7], (FF, D), FF ** -0.5, 0.09375, ((0, 16), (1, 2)), jnp.float32)
    modulate_weight = bell_draw(streams_of[8], (D, 6 * D), D ** -0.5, 0.1875, ((0, 16), (1, 2)), jnp.float32)
    entry_velocity = bell_draw(streams_of[9], (D, 3 * D), (0.3 * (LATENTS * P_SIZE) ** 0.5), 160.0, ((0, 16), (1, 2)), jnp.float32)
    merge_velocity = bell_draw(streams_of[10], (D, D), (0.3 * (LATENTS * P_SIZE) ** 0.5), 160.0, ((0, 16), (1, 2)), jnp.float32)
    expand_velocity = bell_draw(streams_of[11], (D, FF), (0.3 * (LATENTS * P_SIZE) ** 0.5), 160.0, ((0, 16), (1, 2)), jnp.float32)
    shrink_velocity = bell_draw(streams_of[12], (FF, D), (0.3 * (LATENTS * P_SIZE) ** 0.5), 160.0, ((0, 16), (1, 2)), jnp.float32)
    modulate_velocity = bell_draw(streams_of[13], (D, 6 * D), (0.3 * (LATENTS * P_SIZE) ** 0.5), 160.0, ((0, 16), (1, 2)), jnp.float32)
    entry_average = bell_draw(streams_of[14], (D, 3 * D), D ** -0.5, 0.1875, ((0, 16), (1, 2)), jnp.float32)
    merge_average = bell_draw(streams_of[15], (D, D), (D // 32) ** -0.5, 1.0, ((0, 16), (1, 2)), jnp.float32)
    expand_average = bell_draw(streams_of[16], (D, FF), D ** -0.5, 0.1875, ((0, 16), (1, 2)), jnp.float32)
    shrink_average = bell_draw(streams_of[17], (FF, D), FF ** -0.5, 0.09375, ((0, 16), (1, 2)), jnp.float32)
    modulate_average = bell_draw(streams_of[18], (D, 6 * D), D ** -0.5, 0.1875, ((0, 16), (1, 2)), jnp.float32)
    return dict(tokens=tokens, condition=condition, kept_tokens=kept_tokens, grad_out=grad_out, entry_weight=entry_weight, merge_weight=merge_weight, expand_weight=expand_weight, shrink_weight=shrink_weight, modulate_weight=modulate_weight, entry_velocity=entry_velocity, merge_velocity=merge_velocity, expand_velocity=expand_velocity, shrink_velocity=shrink_velocity, modulate_velocity=modulate_velocity, entry_average=entry_average, merge_average=merge_average, expand_average=expand_average, shrink_average=shrink_average, modulate_average=modulate_average)


@jax.custom_vjp
def low(v):
    return lax.optimization_barrier(v.astype(jnp.bfloat16)).astype(jnp.float32)

@jax.custom_vjp
def low_back(v):
    return v

def low_keep(v):
    return (low(v), None)

def low_pass(kept, grad):
    return (grad,)

def back_keep(v):
    return (v, None)

def back_low(kept, grad):
    return (low(grad),)
low.defvjp(low_keep, low_pass)
low_back.defvjp(back_keep, back_low)

def matmul(left, right):
    return jnp.dot(left, right, precision=lax.Precision.HIGHEST)

def normalize(values):
    average = lax.optimization_barrier(jnp.mean(values, axis=-1, keepdims=True))
    centred = values - average
    return centred * lax.rsqrt(lax.optimization_barrier(jnp.mean(centred * centred, axis=-1, keepdims=True)) + 1e-06)

def block(tokens, condition, kept_tokens, entry, merge, expand, shrink, modulate):
    latents, length, model_width = tokens.shape
    head_size = model_width // HEADS
    lifted = low(jax.nn.silu(condition))
    table = low_back(matmul(lifted, low(modulate))).reshape(latents, 6, model_width)
    shift_one = table[:, 0][:, None, :]
    scale_one = table[:, 1][:, None, :]
    gate_one = table[:, 2][:, None, :]
    shift_two = table[:, 3][:, None, :]
    scale_two = table[:, 4][:, None, :]
    gate_two = table[:, 5][:, None, :]
    kept_mask = kept_tokens.astype(jnp.float32)[:, :, None]
    hidden_one = low(normalize(tokens) * (1.0 + scale_one) + shift_one)
    projected = low(low_back(matmul(hidden_one.reshape(-1, model_width), low(entry))))
    sections = projected.reshape(latents, length, 3, HEADS, head_size)
    queries = sections[:, :, 0]
    keys_part = sections[:, :, 1]
    values = sections[:, :, 2]
    raw_scores = jnp.einsum('gqhd,gkhd->ghqk', queries, keys_part, precision=lax.Precision.HIGHEST) / math.sqrt(head_size)
    scores = jnp.where(kept_tokens[:, None, None, :] > 0, low_back(raw_scores), -1000000000.0)
    soft_weights = jax.nn.softmax(scores, axis=-1)
    attended = low(low_back(jnp.einsum('ghqk,gkhd->gqhd', low(soft_weights), values, precision=lax.Precision.HIGHEST)))
    attention_out = low_back(matmul(attended.reshape(-1, model_width), low(merge))).reshape(latents, length, model_width)
    middle = tokens + kept_mask * gate_one * attention_out
    hidden_two = low(normalize(middle) * (1.0 + scale_two) + shift_two)
    expanded = low_back(matmul(hidden_two.reshape(-1, model_width), low(expand)))
    activated = low(jax.nn.gelu(expanded))
    feed = low_back(matmul(activated, low(shrink))).reshape(latents, length, model_width)
    return middle + kept_mask * gate_two * feed

def reference(tokens, condition, kept_tokens, grad_out, entry_weight, merge_weight, expand_weight, shrink_weight, modulate_weight, entry_velocity, merge_velocity, expand_velocity, shrink_velocity, modulate_velocity, entry_average, merge_average, expand_average, shrink_average, modulate_average):
    masters = (entry_weight, merge_weight, expand_weight, shrink_weight, modulate_weight)
    velocities = (entry_velocity, merge_velocity, expand_velocity, shrink_velocity, modulate_velocity)
    averages = (entry_average, merge_average, expand_average, shrink_average, modulate_average)
    group_size = math.gcd(LATENTS, max(1, 4096 // P_SIZE))
    rounds = LATENTS // group_size

    def regroup(values):
        return values.reshape((rounds, group_size) + values.shape[1:])

    def accumulate(carry, bundle):
        block_tokens, block_condition, block_kept, block_grad = bundle

        def run_block(inputs, *weights):
            return block(inputs, block_condition, block_kept, *weights)
        result, pullback = jax.vjp(run_block, block_tokens, *masters)
        gradients = pullback(block_grad)
        carry = tuple((running + fresh for running, fresh in zip(carry, gradients[1:])))
        return (carry, (result, gradients[0]))
    initial = tuple((jnp.zeros_like(master) for master in masters))
    totals, (results, input_grads) = lax.scan(accumulate, initial, (regroup(tokens), regroup(condition), regroup(kept_tokens), regroup(grad_out)))
    rate = 0.03 / math.sqrt(LATENTS * P_SIZE)
    moved_list = []
    velocity_list = []
    average_list = []
    for master, velocity, average, gradient in zip(masters, velocities, averages, totals):
        fresh_velocity = 0.5 * velocity + gradient
        moved = master - rate * (gradient + 0.5 * fresh_velocity)
        moved_list.append(moved)
        velocity_list.append(fresh_velocity)
        average_list.append(0.5 * average + 0.5 * moved)
    return (results.reshape(tokens.shape), input_grads.reshape(tokens.shape), moved_list[0], moved_list[1], moved_list[2], moved_list[3], moved_list[4], velocity_list[0], velocity_list[1], velocity_list[2], velocity_list[3], velocity_list[4], average_list[0], average_list[1], average_list[2], average_list[3], average_list[4])
```

```python
import math

import jax
import jax.numpy as jnp
from jax import lax
from jax.experimental import pallas as pl
from jax.experimental.pallas import tpu as pltpu
from jax.sharding import PartitionSpec as P

HEADS = 16
EPSILON = 1e-06
DECAY = 0.5
BF = jnp.bfloat16
F32 = jnp.float32


def normalize(values):
    average = jnp.mean(values, axis=-1, keepdims=True)
    centred = values - average
    inverse = lax.rsqrt(jnp.mean(centred * centred, axis=-1, keepdims=True) + EPSILON)
    return (centred * inverse, inverse)


def norm_back(gradient, normed, inverse):
    return inverse * (
        gradient
        - jnp.mean(gradient, axis=-1, keepdims=True)
        - normed * jnp.mean(gradient * normed, axis=-1, keepdims=True)
    )


def place_kernel(count, depth, order, *refs):
    blocks, out, sems = refs[:count], refs[count], refs[count + 1]
    copies = []
    for b in range(count):
        for i in range(depth):
            at = b * depth + i
            copies.append(pltpu.make_async_copy(blocks[b].at[i], out.at[order[at]], sems.at[at]))
    for copy in copies:
        copy.start()
    for copy in copies:
        copy.wait()


def pick_kernel(count, depth, order, whole, *refs):
    blocks, sems = refs[:count], refs[count]
    copies = []
    for b in range(count):
        for i in range(depth):
            at = b * depth + i
            copies.append(pltpu.make_async_copy(whole.at[order[at]], blocks[b].at[i], sems.at[at]))
    for copy in copies:
        copy.start()
    for copy in copies:
        copy.wait()


def place(blocks, order):
    count, (depth, rows, columns) = len(blocks), blocks[0].shape
    total = count * depth
    return pl.pallas_call(
        lambda *refs: place_kernel(count, depth, *refs),
        out_shape=jax.ShapeDtypeStruct((total, rows, columns), blocks[0].dtype),
        in_specs=[pl.BlockSpec(memory_space=pltpu.SMEM)] + [pl.BlockSpec(memory_space=pl.ANY)] * count,
        out_specs=pl.BlockSpec(memory_space=pltpu.VMEM),
        scratch_shapes=[pltpu.SemaphoreType.DMA((total,))],
        compiler_params=pltpu.CompilerParams(vmem_limit_bytes=48 * 2**20),
        cost_estimate=pl.CostEstimate(
            flops=0, bytes_accessed=4 * total * rows * columns, transcendentals=0
        ),
        name="place",
    )(order, *blocks)


def pick(whole, order, count):
    total, rows, columns = whole.shape
    depth = total // count
    return pl.pallas_call(
        lambda *refs: pick_kernel(count, depth, *refs),
        out_shape=[jax.ShapeDtypeStruct((depth, rows, columns), whole.dtype)] * count,
        in_specs=[pl.BlockSpec(memory_space=pltpu.SMEM), pl.BlockSpec(memory_space=pltpu.VMEM)],
        out_specs=[pl.BlockSpec(memory_space=pl.ANY)] * count,
        scratch_shapes=[pltpu.SemaphoreType.DMA((total,))],
        compiler_params=pltpu.CompilerParams(vmem_limit_bytes=48 * 2**20),
        cost_estimate=pl.CostEstimate(
            flops=0, bytes_accessed=4 * total * rows * columns, transcendentals=0
        ),
        name="pick",
    )(order, whole)


class Grid:
    def __init__(self, seq, dp):
        self.size = {"z": 4, "y": seq // 8, "c": 2, "x": dp}
        assert seq % 8 == 0
        at, column = lax.axis_index("seq"), lax.axis_index("dp")
        sizes = self.size
        self.at = {
            "z": at // (2 * sizes["y"]),
            "y": (at // 2) % sizes["y"],
            "c": at % 2,
            "x": column,
        }

    def send(self, value, axis, shift):
        sizes = self.size
        pairs = []
        for z in range(sizes["z"]):
            for y in range(sizes["y"]):
                for c in range(2):
                    for x in range(sizes["x"]):
                        here = {"z": z, "y": y, "c": c, "x": x}
                        there = dict(here)
                        there[axis] = (here[axis] + shift) % sizes[axis]
                        pairs.append((self.flat(here), self.flat(there)))
        return lax.ppermute(value, ("seq", "dp"), pairs)

    def flat(self, p):
        sizes = self.size
        return ((p["z"] * sizes["y"] + p["y"]) * 2 + p["c"]) * sizes["x"] + p["x"]

    def swap(self, value):
        return self.send(value, "c", 1)

    def off(self, axis, shift):
        return (self.at[axis] + shift) % self.size[axis]


def gather_small(grid, value, axes):
    for axis in axes:
        value = jnp.stack(
            [value] + [grid.send(value, axis, shift) for shift in range(1, grid.size[axis])]
        )
    return value


def to_order(grid, values, axis):
    count = len(values)
    line = jnp.stack(values + values[:-1])
    return lax.dynamic_slice_in_dim(line, (count - grid.at[axis]) % count, count, axis=0)


def gather_part(grid, piece, last):
    sizes = grid.size
    stack = jnp.stack([piece] + [grid.send(piece, "z", shift) for shift in range(1, sizes["z"])])
    if sizes["x"] > 2:
        line = [stack] + [grid.send(stack, "y", shift) for shift in range(1, sizes["y"])]
        whole = lax.all_gather(jnp.stack(line), "dp", axis=0)
        return [whole[x, sy] for x in range(sizes["x"]) for sy in range(sizes["y"])]
    first = "y" if last == "x" else "x"
    blocks = {(0, 0): stack}
    for shift in range(1, sizes[first]):
        blocks[(shift, 0)] = grid.send(stack, first, shift)
    for shift in range(sizes[first]):
        for far in range(1, sizes[last]):
            blocks[(shift, far)] = grid.send(blocks[(shift, 0)], last, far)
    if first == "x":
        return [blocks[(sx, sy)] for sx in range(sizes["x"]) for sy in range(sizes["y"])]
    return [blocks[(sy, sx)] for sx in range(sizes["x"]) for sy in range(sizes["y"])]


def scatter_part(grid, blocks, last):
    sizes = grid.size
    if sizes["x"] > 2:
        pairs = jnp.stack(blocks).reshape((sizes["x"], sizes["y"]) + blocks[0].shape)
        kept = lax.psum_scatter(pairs, "dp", scatter_dimension=0).astype(F32)
        return scatter_line(grid, [kept[sy] for sy in range(sizes["y"])], "y")
    at = {}
    it = iter(blocks)
    for sx in range(sizes["x"]):
        for sy in range(sizes["y"]):
            at[(sx, sy) if last == "y" else (sy, sx)] = next(it)
    first = "y" if last == "x" else "x"
    kept = []
    for near in range(sizes[first] - 1, -1, -1):
        total = at[(near, 0)].astype(F32)
        for far in range(1, sizes[last]):
            total = total + grid.send(at[(near, far)], last, far).astype(F32)
        kept.append(total)
    return scatter_line(grid, kept[::-1], first)


def scatter_line(grid, kept, axis):
    sizes = grid.size
    total = kept[0]
    for near in range(1, sizes[axis]):
        total = total + grid.send(kept[near].astype(BF), axis, near).astype(F32)
    result = total[0]
    for shift in range(1, sizes["z"]):
        result = result + grid.send(total[shift].astype(BF), "z", shift).astype(F32)
    return result


def orders(grid, sign, parts):
    sizes = grid.size
    result = []
    for part in parts:
        for sx in range(sizes["x"]):
            for sy in range(sizes["y"]):
                for sz in range(sizes["z"]):
                    x = grid.off("x", sign * sx) if sizes["x"] == 2 else sx
                    y = grid.off("y", sign * sy)
                    z = grid.off("z", sign * sz)
                    result.append(((x * sizes["z"] + z) * sizes["y"] + y) * len(parts) + part)
    return jnp.stack(result).astype(jnp.int32)


def gather(grid, pieces, lasts, parts):
    blocks = []
    for piece, last in zip(pieces, lasts):
        blocks += gather_part(grid, piece, last)
    rows, columns = pieces[0].shape
    whole = place(blocks, orders(grid, -1, parts))
    return whole.reshape(grid.size["x"], -1, columns)


def scatter(grid, whole, rows, lasts, parts):
    columns = whole.shape[-1]
    sizes = grid.size
    count = len(parts) * sizes["x"] * sizes["y"]
    blocks = pick(whole.astype(BF).reshape(-1, rows, columns), orders(grid, 1, parts), count)
    each = count // len(parts)
    return [
        scatter_part(grid, blocks[i * each : (i + 1) * each], last) for i, last in enumerate(lasts)
    ]


def heads_of(grid, whole, rows, head_size):
    if rows % head_size == 0:
        return whole
    assert head_size == 2 * rows
    first = grid.at["c"] == 0
    halves = whole.reshape(whole.shape[0], HEADS // 2, 2, rows, -1)
    even, odd = halves[:, :, 0], halves[:, :, 1]
    kept = jnp.where(first, even, odd)
    came = grid.swap(jnp.where(first, odd, even))
    low, high = jnp.where(first, kept, came), jnp.where(first, came, kept)
    return jnp.stack([low, high], axis=2).reshape(whole.shape)


def rows_of(grid, whole, rows, head_size):
    if rows % head_size == 0:
        return whole
    first = grid.at["c"] == 0
    halves = whole.reshape(whole.shape[0], HEADS // 2, 2, rows, -1)
    low, high = halves[:, :, 0], halves[:, :, 1]
    kept = jnp.where(first, low, high)
    came = grid.swap(jnp.where(first, high, low))
    even, odd = jnp.where(first, kept, came), jnp.where(first, came, kept)
    return jnp.stack([even, odd], axis=2).reshape(whole.shape)


def split_core(grid, weight, block):
    rows, columns = weight.shape
    pairs = weight.reshape(rows, columns // (2 * block), 2, block)
    even = pairs[:, :, 0].reshape(rows, -1)
    odd = pairs[:, :, 1].reshape(rows, -1)
    first = grid.at["c"] == 0
    return (jnp.where(first, even, odd), jnp.where(first, odd, even))


def join_core(grid, own, other, block):
    rows, columns = own.shape
    first = grid.at["c"] == 0
    even = jnp.where(first, own, other).reshape(rows, -1, 1, block)
    odd = jnp.where(first, other, own).reshape(rows, -1, 1, block)
    return jnp.concatenate([even, odd], axis=2).reshape(rows, 2 * columns)


def attend(projected, kept):
    group, length, triple = projected.shape
    width = triple // 3
    head_size = width // (HEADS // 2)
    sections = projected.reshape(group, length, 3, HEADS // 2, head_size)
    queries, keys_part, values = sections[:, :, 0], sections[:, :, 1], sections[:, :, 2]
    scale = 1.0 / math.sqrt(head_size)
    scores = (
        jnp.einsum("gqhd,gkhd->ghqk", queries, keys_part, preferred_element_type=F32) * scale
    )
    scores = jnp.where(kept[:, None, None, :] > 0, scores, -1000000000.0)
    row_max = jnp.max(scores, axis=-1, keepdims=True)
    exponent = jnp.exp(scores - row_max)
    soft = exponent / jnp.sum(exponent, axis=-1, keepdims=True)
    attended = jnp.einsum("ghqk,gkhd->gqhd", soft.astype(BF), values, preferred_element_type=F32)
    return (attended.astype(BF).reshape(group * length, width), soft)


def attend_back(projected, soft, grad_attended):
    group, length, triple = projected.shape
    width = triple // 3
    head_size = width // (HEADS // 2)
    sections = projected.reshape(group, length, 3, HEADS // 2, head_size)
    queries, keys_part, values = sections[:, :, 0], sections[:, :, 1], sections[:, :, 2]
    scale = 1.0 / math.sqrt(head_size)
    upstream = grad_attended.reshape(group, length, HEADS // 2, head_size)
    grad_soft = jnp.einsum("gqhd,gkhd->ghqk", upstream, values, preferred_element_type=F32)
    grad_scores = (soft * (grad_soft - jnp.sum(soft * grad_soft, axis=-1, keepdims=True))).astype(BF)
    grad_queries = (
        jnp.einsum("ghqk,gkhd->gqhd", grad_scores, keys_part, preferred_element_type=F32) * scale
    )
    grad_keys = (
        jnp.einsum("ghqk,gqhd->gkhd", grad_scores, queries, preferred_element_type=F32) * scale
    )
    grad_values = jnp.einsum(
        "ghqk,gqhd->gkhd", soft.astype(BF), upstream, preferred_element_type=F32
    )
    stacked = jnp.stack([grad_queries, grad_keys, grad_values], axis=2).astype(BF)
    return stacked.reshape(group * length, triple)


def times(rows, weight):
    out = jnp.einsum("tr,xrk->txk", rows, weight, preferred_element_type=F32)
    return out.reshape(out.shape[0], -1)


def times_back(grads, weight):
    split = grads.reshape(grads.shape[0], weight.shape[0], weight.shape[2])
    return jnp.einsum("txk,xrk->tr", split, weight, preferred_element_type=F32)


def outer(rows, grads, count):
    split = grads.reshape(grads.shape[0], count, -1)
    return jnp.einsum("tr,txk->xrk", rows, split, preferred_element_type=F32).astype(BF)


def local(seq, dp, *arguments):
    tokens, condition, kept_tokens, grad_out = arguments[:4]
    masters, velocities, averages = arguments[4:9], arguments[9:14], arguments[14:19]
    entry_own, merge_own, expand_own, shrink_own, modulate_own = [
        master.astype(BF) for master in masters
    ]
    grid = Grid(seq, dp)
    latents, length, width = tokens.shape
    head_size = width // HEADS
    both = 2 * latents
    rows = latents * length
    core = grid.at["c"]
    x_count = grid.size["x"]

    lifted = jax.nn.silu(condition).astype(BF)
    every_lifted = gather_small(grid, lifted, "xcyz")
    part_rows = modulate_own.shape[0]
    my_lifted = lax.dynamic_slice_in_dim(
        every_lifted, lax.axis_index("seq") * part_rows, part_rows, axis=-1
    )
    partial = jnp.einsum("zycxlr,re->zycxle", my_lifted, modulate_own, preferred_element_type=F32)
    for axis in "zyc":
        total = partial[0]
        for shift in range(1, grid.size[axis]):
            total = total + grid.send(partial[shift], axis, -shift)
        partial = total
    mine = [partial[0]] + [grid.send(partial[shift], "x", -shift) for shift in range(1, dp)]
    table = to_order(grid, mine, "x")
    table = jnp.moveaxis(table, 0, 1).reshape(latents, 6, width)
    shift_one, scale_one, gate_one, shift_two, scale_two, gate_two = [
        table[:, number][:, None, :] for number in range(6)
    ]

    ff_block = shrink_own.shape[0]
    entry_mine, entry_theirs = split_core(grid, entry_own, head_size)
    expand_mine, expand_theirs = split_core(grid, expand_own, ff_block)
    entry_other = grid.swap(entry_theirs)
    expand_other = grid.swap(expand_theirs)
    core_parts = (core, 1 - core)
    half = ff_block // 2
    entry = gather(grid, (entry_mine, entry_other), "xy", core_parts)
    merge = heads_of(grid, gather(grid, (merge_own,), "x", (0,)), part_rows, head_size)
    expand = gather(grid, (expand_mine, expand_other), "xy", core_parts)
    shrink = gather(grid, (shrink_own[:half], shrink_own[half:]), "xy", (0, 1))

    kept_mask = kept_tokens.astype(F32)
    kept_both = jnp.concatenate([kept_mask, grid.swap(kept_mask)])
    kept_mask = kept_mask[:, :, None]

    def share(value):
        flat = value.reshape(rows, -1)
        return jnp.concatenate([flat, grid.swap(flat)])

    def settle(value):
        return (value[:rows] + grid.swap(value[rows:])).reshape(latents, length, -1)

    grad_feed = share((kept_mask * gate_two * grad_out).astype(BF))
    normed_one, inverse_one = normalize(tokens)
    hidden_one = share((normed_one * (1.0 + scale_one) + shift_one).astype(BF))
    projected = times(hidden_one, entry).astype(BF).reshape(both, length, -1)
    attended, soft = attend(projected, kept_both)
    attention_out = settle(times(attended, merge))
    middle = tokens + kept_mask * gate_one * attention_out
    normed_two, inverse_two = normalize(middle)
    hidden_two = share((normed_two * (1.0 + scale_two) + shift_two).astype(BF))
    expanded = times(hidden_two, expand)
    activated = jax.nn.gelu(expanded).astype(BF)
    feed = settle(times(activated, shrink))
    result = middle + kept_mask * gate_two * feed

    grad_gate_two = jnp.sum(kept_mask * feed * grad_out, axis=1)
    grad_shrink = outer(activated, grad_feed, x_count)
    shrink_sums = scatter(grid, grad_shrink, half, "xy", (0, 1))
    grad_activated = times_back(grad_feed, shrink)
    grad_expanded = jax.vjp(jax.nn.gelu, expanded)[1](grad_activated)[0].astype(BF)
    grad_expand = outer(hidden_two, grad_expanded, x_count)
    expand_sums = scatter(grid, grad_expand, part_rows, "xy", core_parts)
    grad_hidden_two = settle(times_back(grad_expanded, expand))
    grad_scale_two = jnp.sum(grad_hidden_two * normed_two, axis=1)
    grad_shift_two = jnp.sum(grad_hidden_two, axis=1)
    grad_middle = grad_out + norm_back(grad_hidden_two * (1.0 + scale_two), normed_two, inverse_two)
    grad_attention = share((kept_mask * gate_one * grad_middle).astype(BF))
    grad_gate_one = jnp.sum(kept_mask * attention_out * grad_middle, axis=1)
    grad_merge = outer(attended, grad_attention, x_count)
    grad_merge = rows_of(grid, grad_merge, part_rows, head_size)
    merge_sums = scatter(grid, grad_merge, part_rows, "x", (0,))
    grad_attended = times_back(grad_attention, merge).astype(BF)
    grad_projected = attend_back(projected, soft, grad_attended)
    grad_entry = outer(hidden_one, grad_projected, x_count)
    entry_sums = scatter(grid, grad_entry, part_rows, "xy", core_parts)
    grad_hidden_one = settle(times_back(grad_projected, entry))
    grad_scale_one = jnp.sum(grad_hidden_one * normed_one, axis=1)
    grad_shift_one = jnp.sum(grad_hidden_one, axis=1)
    grad_tokens = grad_middle + norm_back(
        grad_hidden_one * (1.0 + scale_one), normed_one, inverse_one
    )
    grad_table = jnp.concatenate(
        [
            grad_shift_one,
            grad_scale_one,
            grad_gate_one,
            grad_shift_two,
            grad_scale_two,
            grad_gate_two,
        ],
        axis=1,
    ).astype(BF)
    columns = modulate_own.shape[1]
    away = [
        lax.dynamic_slice_in_dim(grad_table, grid.off("x", shift) * columns, columns, axis=1)
        for shift in range(dp)
    ]
    for_me = jnp.stack(
        [away[0]] + [grid.send(away[shift], "x", shift) for shift in range(1, dp)]
    )
    every_table = gather_small(grid, for_me, "cyz")
    modulate_sum = jnp.einsum(
        "zycxlr,zycxle->re", my_lifted, every_table, preferred_element_type=F32
    )

    entry_sum = join_core(grid, entry_sums[0], grid.swap(entry_sums[1]), head_size)
    expand_sum = join_core(grid, expand_sums[0], grid.swap(expand_sums[1]), ff_block)
    shrink_sum = jnp.concatenate(shrink_sums)
    summed = (entry_sum, merge_sums[0], expand_sum, shrink_sum, modulate_sum)

    rate = 0.03 / math.sqrt(rows * seq * dp)
    moved_list = []
    velocity_list = []
    average_list = []
    for master, velocity, average, gradient in zip(masters, velocities, averages, summed):
        fresh_velocity = DECAY * velocity + gradient
        moved = master - rate * (gradient + DECAY * fresh_velocity)
        moved_list.append(moved)
        velocity_list.append(fresh_velocity)
        average_list.append(0.5 * average + 0.5 * moved)
    return (result, grad_tokens) + tuple(moved_list) + tuple(velocity_list) + tuple(average_list)


def solution(mesh):
    spread = P(("seq", "dp"), None, None)
    flat = P(("seq", "dp"), None)
    weight = P("seq", "dp")
    seq, dp = mesh.shape["seq"], mesh.shape["dp"]
    return jax.shard_map(
        lambda *arguments: local(seq, dp, *arguments),
        mesh=mesh,
        in_specs=(spread, flat, flat, spread) + (weight,) * 15,
        out_specs=(spread, spread) + (weight,) * 15,
        check_vma=False,
    )
```

```python
import math

import jax
import jax.numpy as jnp
from jax import lax
from jax.experimental import pallas as pl
from jax.experimental.pallas import tpu as pltpu
from jax.sharding import PartitionSpec as P

HEADS = 16
EPSILON = 1e-06
DECAY = 0.5
BF = jnp.bfloat16
F32 = jnp.float32


def normalize(values):
    average = jnp.mean(values, axis=-1, keepdims=True)
    centred = values - average
    inverse = lax.rsqrt(jnp.mean(centred * centred, axis=-1, keepdims=True) + EPSILON)
    return (centred * inverse, inverse)


def norm_back(gradient, normed, inverse):
    return inverse * (
        gradient
        - jnp.mean(gradient, axis=-1, keepdims=True)
        - normed * jnp.mean(gradient * normed, axis=-1, keepdims=True)
    )


def place_kernel(count, depth, order, *refs):
    blocks, out, sems = refs[:count], refs[count], refs[count + 1]
    copies = []
    for b in range(count):
        for i in range(depth):
            at = b * depth + i
            copies.append(pltpu.make_async_copy(blocks[b].at[i], out.at[order[at]], sems.at[at]))
    for copy in copies:
        copy.start()
    for copy in copies:
        copy.wait()


def pick_kernel(count, depth, order, whole, *refs):
    blocks, sems = refs[:count], refs[count]
    copies = []
    for b in range(count):
        for i in range(depth):
            at = b * depth + i
            copies.append(pltpu.make_async_copy(whole.at[order[at]], blocks[b].at[i], sems.at[at]))
    for copy in copies:
        copy.start()
    for copy in copies:
        copy.wait()


def place(blocks, order):
    count, (depth, rows, columns) = len(blocks), blocks[0].shape
    total = count * depth
    return pl.pallas_call(
        lambda *refs: place_kernel(count, depth, *refs),
        out_shape=jax.ShapeDtypeStruct((total, rows, columns), blocks[0].dtype),
        in_specs=[pl.BlockSpec(memory_space=pltpu.SMEM)] + [pl.BlockSpec(memory_space=pl.ANY)] * count,
        out_specs=pl.BlockSpec(memory_space=pltpu.VMEM),
        scratch_shapes=[pltpu.SemaphoreType.DMA((total,))],
        compiler_params=pltpu.CompilerParams(vmem_limit_bytes=48 * 2**20),
        cost_estimate=pl.CostEstimate(
            flops=0, bytes_accessed=4 * total * rows * columns, transcendentals=0
        ),
        name="place",
    )(order, *blocks)


def pick(whole, order, count):
    total, rows, columns = whole.shape
    depth = total // count
    return pl.pallas_call(
        lambda *refs: pick_kernel(count, depth, *refs),
        out_shape=[jax.ShapeDtypeStruct((depth, rows, columns), whole.dtype)] * count,
        in_specs=[pl.BlockSpec(memory_space=pltpu.SMEM), pl.BlockSpec(memory_space=pltpu.VMEM)],
        out_specs=[pl.BlockSpec(memory_space=pl.ANY)] * count,
        scratch_shapes=[pltpu.SemaphoreType.DMA((total,))],
        compiler_params=pltpu.CompilerParams(vmem_limit_bytes=48 * 2**20),
        cost_estimate=pl.CostEstimate(
            flops=0, bytes_accessed=4 * total * rows * columns, transcendentals=0
        ),
        name="pick",
    )(order, whole)


class Grid:
    def __init__(self, seq, dp):
        self.size = {"z": 4, "y": seq // 8, "c": 2, "x": dp}
        assert seq % 8 == 0
        at, column = lax.axis_index("seq"), lax.axis_index("dp")
        sizes = self.size
        self.at = {
            "z": at // (2 * sizes["y"]),
            "y": (at // 2) % sizes["y"],
            "c": at % 2,
            "x": column,
        }

    def send(self, value, axis, shift):
        sizes = self.size
        pairs = []
        for z in range(sizes["z"]):
            for y in range(sizes["y"]):
                for c in range(2):
                    for x in range(sizes["x"]):
                        here = {"z": z, "y": y, "c": c, "x": x}
                        there = dict(here)
                        there[axis] = (here[axis] + shift) % sizes[axis]
                        pairs.append((self.flat(here), self.flat(there)))
        return lax.ppermute(value, ("seq", "dp"), pairs)

    def flat(self, p):
        sizes = self.size
        return ((p["z"] * sizes["y"] + p["y"]) * 2 + p["c"]) * sizes["x"] + p["x"]

    def swap(self, value):
        return self.send(value, "c", 1)

    def off(self, axis, shift):
        return (self.at[axis] + shift) % self.size[axis]


barrier = lax.optimization_barrier


def gather_plain(grid, piece):
    sizes = grid.size
    stack = jnp.stack([piece] + [grid.send(piece, "z", shift) for shift in range(1, sizes["z"])])
    line = [stack] + [grid.send(stack, "y", shift) for shift in range(1, sizes["y"])]
    whole = lax.all_gather(jnp.stack(line), "dp", axis=0)
    blocks = [whole[x, sy] for x in range(sizes["x"]) for sy in range(sizes["y"])]
    order = plain_order(grid, -1)
    return place(blocks, order).reshape(sizes["x"], -1, piece.shape[1])


def scatter_plain(grid, whole, rows):
    sizes = grid.size
    count = sizes["x"] * sizes["y"]
    blocks = pick(whole.reshape(-1, rows, whole.shape[-1]), plain_order(grid, 1), count)
    pairs = jnp.stack(blocks).reshape((sizes["x"], sizes["y"]) + blocks[0].shape)
    kept = lax.psum_scatter(pairs, "dp", scatter_dimension=0).astype(F32)
    total = kept[0]
    for near in range(1, sizes["y"]):
        total = total + grid.send(kept[near].astype(BF), "y", near).astype(F32)
    return scatter_z(grid, total)


def scatter_z(grid, total):
    result = total[0]
    for shift in range(1, grid.size["z"]):
        result = result + grid.send(total[shift].astype(BF), "z", shift).astype(F32)
    return result


def plain_order(grid, sign):
    sizes = grid.size
    result = []
    for x in range(sizes["x"]):
        for sy in range(sizes["y"]):
            for sz in range(sizes["z"]):
                y, z = grid.off("y", sign * sy), grid.off("z", sign * sz)
                result.append((x * sizes["z"] + z) * sizes["y"] + y)
    return jnp.stack(result).astype(jnp.int32)


def along_z(grid, piece):
    return [grid.send(piece, "z", shift) for shift in range(1, grid.size["z"])]


def to_near(grid, stack):
    return [grid.send(stack, axis, 1) for axis in "xy"]


def to_far(grid, near, cut):
    by_x, by_y = near
    return [grid.send(by_y[:, :cut], "x", 1), grid.send(by_x[:, cut:], "y", 1)]


def gathered(grid, stack, near, far, cut):
    blocks = [(stack, 0, 0, 0), (near[1], 0, 1, 0), (near[0], 1, 0, 0)]
    return Weight(grid, blocks + [(far[0], 1, 1, 0), (far[1], 1, 1, cut)])


def scatter_first(grid, blocks):
    _, away_x, _, away_y = blocks
    return [grid.send(away_x, "x", 1), grid.send(away_y, "y", 1)]


def scatter_second(grid, blocks, came):
    kept_x, _, kept_y, _ = blocks
    by_x = (kept_x[1].astype(F32) + came[0][1].astype(F32)).astype(BF)
    by_y = (kept_y[1].astype(F32) + came[1][1].astype(F32)).astype(BF)
    return [grid.send(by_x, "y", 1), grid.send(by_y, "x", 1)]


def scatter_third(grid, blocks, came, more):
    parts = [
        kept[0].astype(F32) + near[0].astype(F32) + far.astype(F32)
        for kept, near, far in zip(blocks[::2], came, more)
    ]
    total = jnp.concatenate(parts, axis=1)
    low = total[1:].astype(BF)
    return total[0], [grid.send(low[shift - 1], "z", shift) for shift in range(1, grid.size["z"])]


def scatter_last(own, came):
    for value in came:
        own = own + value.astype(F32)
    return own


def heads_of(grid, whole, rows, head_size):
    if rows % head_size == 0:
        return whole
    assert head_size == 2 * rows
    first = grid.at["c"] == 0
    halves = whole.reshape(whole.shape[0], HEADS // 2, 2, rows, -1)
    even, odd = halves[:, :, 0], halves[:, :, 1]
    kept = jnp.where(first, even, odd)
    came = grid.swap(jnp.where(first, odd, even))
    low, high = jnp.where(first, kept, came), jnp.where(first, came, kept)
    return jnp.stack([low, high], axis=2).reshape(whole.shape)


def rows_of(grid, whole, rows, head_size):
    if rows % head_size == 0:
        return whole
    first = grid.at["c"] == 0
    halves = whole.reshape(whole.shape[0], HEADS // 2, 2, rows, -1)
    low, high = halves[:, :, 0], halves[:, :, 1]
    kept = jnp.where(first, low, high)
    came = grid.swap(jnp.where(first, high, low))
    even, odd = jnp.where(first, kept, came), jnp.where(first, came, kept)
    return jnp.stack([even, odd], axis=2).reshape(whole.shape)


def split_core(grid, weight, block):
    rows, columns = weight.shape
    pairs = weight.reshape(rows, columns // (2 * block), 2, block)
    even = pairs[:, :, 0].reshape(rows, -1)
    odd = pairs[:, :, 1].reshape(rows, -1)
    first = grid.at["c"] == 0
    return (jnp.where(first, even, odd), jnp.where(first, odd, even))


def join_core(grid, own, other, block):
    rows, columns = own.shape
    first = grid.at["c"] == 0
    even = jnp.where(first, own, other).reshape(rows, -1, 1, block)
    odd = jnp.where(first, other, own).reshape(rows, -1, 1, block)
    return jnp.concatenate([even, odd], axis=2).reshape(rows, 2 * columns)


def chip_rows(grid, own, other):
    first = grid.at["c"] == 0
    return jnp.concatenate([jnp.where(first, own, other), jnp.where(first, other, own)])


def core_rows(grid, summed, block):
    rows = summed.shape[0] // 2
    first = grid.at["c"] == 0
    low, high = summed[:rows], summed[rows:]
    own = jnp.where(first, low, high)
    other = grid.swap(jnp.where(first, high, low))
    return join_core(grid, own, other, block)


GELU_A = 0.7978845608028654
GELU_B = 0.044715


def gelu(v):
    return 0.5 * v * (1.0 + jnp.tanh(GELU_A * (v + GELU_B * (v * v * v))))


def gelu_slope(v):
    inner = jnp.tanh(GELU_A * (v + GELU_B * (v * v * v)))
    return 0.5 * (1.0 + inner) + 0.5 * v * (1.0 - inner * inner) * (
        GELU_A * (1.0 + 3.0 * GELU_B * v * v)
    )


class Weight:
    def __init__(self, grid, blocks):
        self.grid = grid
        self.order = place_of(grid, -1)
        self.blocks = [block[0] for block in blocks]
        self.marks = [block[1:] for block in blocks]
        _, self.tall, wide = self.blocks[0].shape
        sizes = grid.size
        self.shape = (sizes["x"], sizes["z"] * sizes["y"] * self.tall, wide)


def place_of(grid, sign):
    sizes = grid.size
    result = []
    for axis in "xyz":
        result += [grid.off(axis, sign * shift) for shift in range(sizes[axis])]
    return jnp.stack(result).astype(jnp.int32)


def spot(whole, order, mark, sz, tall, rows):
    sx, sy, offset = mark
    x, y, z = order[sx], order[2 + sy], order[4 + sz]
    return whole.at[x, pl.ds(pl.multiple_of((z * 2 + y) * tall + offset, 16), rows), :]


def fill(blocks, order, whole, tall, marks):
    for block, mark in zip(blocks, marks):
        depth, rows, _ = block.shape

        def put(i, carry, block=block, mark=mark, rows=rows):
            spot(whole, order, mark, i, tall, rows)[...] = block[i]
            return carry

        lax.fori_loop(0, depth, put, 0)


def cost(flops, *arrays):
    return pl.CostEstimate(flops=1024, bytes_accessed=1024, transcendentals=0)


def limit(*arrays):
    total = sum(math.prod(a.shape) * jnp.dtype(a.dtype).itemsize for a in arrays)
    return pltpu.CompilerParams(vmem_limit_bytes=min(56 * 2**20, total * 9 // 8 + 16 * 2**20))


STEP = 256


def times_kernel(count, tall, marks, finish, order, rows, *refs):
    blocks, outs, whole = refs[:count], refs[count:-1], refs[-1]
    fill(blocks, order, whole, tall, marks)
    groups, total, depth = rows.shape
    for x in range(whole.shape[0]):
        for start in range(0, total, STEP):
            here = pl.ds(start, STEP)
            value = None
            for a in range(groups):
                part = jnp.dot(
                    rows[a, here, :],
                    whole[x, a * depth : (a + 1) * depth, :],
                    preferred_element_type=F32,
                )
                value = part if value is None else value + part
            finish(x, here, value, outs)


def to_group(x, here, value, outs):
    outs[0][x, here, :] = value.astype(outs[0].dtype)


def to_columns(x, here, value, outs):
    wide = value.shape[1]
    outs[0][here, x * wide : (x + 1) * wide] = value.astype(outs[0].dtype)


def to_gelu(x, here, value, outs):
    outs[0][x, here, :] = value
    outs[1][x, here, :] = gelu(value).astype(BF)


def fused(kernel, name, weight, flops, outs, before, after=()):
    blocks = weight.blocks
    whole = jax.ShapeDtypeStruct(weight.shape, BF)
    vm = pl.BlockSpec(memory_space=pltpu.VMEM)
    return pl.pallas_call(
        lambda *refs: kernel(len(blocks), weight.tall, weight.marks, *refs),
        out_shape=outs,
        in_specs=[pl.BlockSpec(memory_space=pltpu.SMEM)]
        + [vm] * (len(before) + len(blocks) + len(after)),
        out_specs=[vm] * len(outs),
        scratch_shapes=[pltpu.VMEM(weight.shape, BF)],
        compiler_params=limit(whole, whole, *before, *after, *outs),
        cost_estimate=cost(flops, whole, *before, *after, *outs),
        name=name,
    )(weight.order, *before, *blocks, *after)


def times(rows, weight, kind):
    if not isinstance(weight, Weight):
        return times_plain(rows, weight, kind)
    groups, total, depth = rows.shape
    x_count, tall, wide = weight.shape
    flops = 2 * total * tall * wide * x_count
    if kind == "gelu":
        finish = to_gelu
        outs = [
            jax.ShapeDtypeStruct((x_count, total, wide), F32),
            jax.ShapeDtypeStruct((x_count, total, wide), BF),
        ]
    elif kind == "group":
        finish, outs = to_group, [jax.ShapeDtypeStruct((x_count, total, wide), BF)]
    else:
        finish, outs = to_columns, [jax.ShapeDtypeStruct((total, x_count * wide), F32)]

    def kernel(count, tall, marks, *refs):
        times_kernel(count, tall, marks, finish, *refs)

    result = fused(kernel, "times", weight, flops, outs, (rows,))
    return result if len(result) > 1 else result[0]


def back_kernel(count, tall, marks, order, grads, *refs):
    blocks = refs[:count]
    whole, rest = refs[-1], refs[count:-1]
    out, slope = rest[-1], (rest[0] if len(rest) > 1 else None)
    fill(blocks, order, whole, tall, marks)
    x_count, depth, wide = whole.shape
    groups, total, part = out.shape
    for a in range(groups):
        for start in range(0, total, STEP):
            here = pl.ds(start, STEP)
            value = None
            for x in range(x_count):
                if len(grads.shape) == 3:
                    left = grads[x, here, :]
                else:
                    left = grads[here, x * wide : (x + 1) * wide]
                term = lax.dot_general(
                    left,
                    whole[x, a * part : (a + 1) * part, :],
                    (((1,), (1,)), ((), ())),
                    preferred_element_type=F32,
                )
                value = term if value is None else value + term
            if slope is not None:
                value = value * gelu_slope(slope[a, here, :])
            out[a, here, :] = value.astype(out.dtype)


def times_back(grads, weight, groups, kind, slope=None):
    if not isinstance(weight, Weight):
        return times_back_plain(grads, weight, groups, kind, slope)
    x_count, tall, wide = weight.shape
    total = grads.shape[-2]
    flops = 2 * total * tall * wide * x_count
    outs = [jax.ShapeDtypeStruct((groups, total, tall // groups), kind)]
    after = () if slope is None else (slope,)
    return fused(back_kernel, "times_back", weight, flops, outs, (grads,), after)[0]


def outer_kernel(tall, marks, order, rows, grads, *refs):
    blocks, whole, sems = refs[:-2], refs[-2], refs[-1]
    groups, _, depth = rows.shape
    x_count, _, wide = whole.shape
    for x in range(x_count):
        right = grads[x, :, :] if len(grads.shape) == 3 else grads[:, x * wide : (x + 1) * wide]
        for a in range(groups):
            value = lax.dot_general(
                rows[a, :, :], right, (((0,), (0,)), ((), ())), preferred_element_type=F32
            )
            whole[x, a * depth : (a + 1) * depth, :] = value.astype(BF)
    copies = []
    for block, pair in zip(blocks, marks):
        _, deep, high, _ = block.shape
        for j, mark in enumerate(pair):
            for i in range(deep):
                there = spot(whole, order, mark, i, tall, high)
                sem = sems.at[len(copies)]
                copies.append(pltpu.make_async_copy(there, block.at[j, i], sem))
    for copy in copies:
        copy.start()
    for copy in copies:
        copy.wait()


def outer(grid, rows, grads, tall, cut):
    sizes = grid.size
    groups, total, depth = rows.shape
    x_count = sizes["x"]
    wide = grads.shape[-1] if len(grads.shape) == 3 else grads.shape[1] // x_count
    outs, marks = [], []
    for start, high, by_x in ((0, cut, True), (cut, tall - cut, False)):
        for away in (0, 1):
            if high:
                outs.append(jax.ShapeDtypeStruct((2, sizes["z"], high, wide), BF))
                marks.append(
                    [(away, j, start) if by_x else (j, away, start) for j in range(2)]
                )
    assert groups * depth == sizes["z"] * sizes["y"] * tall
    whole = jax.ShapeDtypeStruct((x_count, groups * depth, wide), BF)
    vm = pl.BlockSpec(memory_space=pltpu.VMEM)
    flops = 2 * total * groups * depth * wide * x_count
    blocks = pl.pallas_call(
        lambda *refs: outer_kernel(tall, marks, *refs),
        out_shape=outs,
        in_specs=[pl.BlockSpec(memory_space=pltpu.SMEM), vm, vm],
        out_specs=[pl.BlockSpec(memory_space=pl.ANY)] * len(outs),
        scratch_shapes=[
            pltpu.VMEM(whole.shape, BF),
            pltpu.SemaphoreType.DMA((len(outs) * 2 * sizes["z"],)),
        ],
        compiler_params=limit(whole, rows, grads),
        cost_estimate=cost(flops, whole, rows, grads),
        name="outer",
    )(place_of(grid, 1), rows, grads)
    return tuple(blocks) + (None,) * (4 - len(blocks))


def head_at(number, head_size, wide):
    start = number * head_size
    return start // wide, start % wide


def soft_of(queries, keys_part, kept):
    scale = 1.0 / math.sqrt(queries.shape[1])
    scores = lax.dot_general(
        queries, keys_part, (((1,), (1,)), ((), ())), preferred_element_type=F32
    )
    scores = jnp.where(kept > 0, scores * scale, -1000000000.0)
    exponent = jnp.exp(scores - jnp.max(scores, axis=-1, keepdims=True))
    return exponent / jnp.sum(exponent, axis=-1, keepdims=True)


def attend_kernel(heads, head_size, padded, projected, kept, attended):
    group, length = kept.shape
    wide = projected.shape[2]

    def part(which, head, here):
        x, at = head_at(which * heads + head, head_size, wide)
        return projected[x, here, at : at + head_size]

    for g in range(group):
        here = pl.ds(g * length, length)
        mask = kept[g : g + 1, :]
        for head in range(heads):
            soft = soft_of(part(0, head, here), part(1, head, here), mask)
            value = jnp.dot(
                soft.astype(BF), part(2, head, here), preferred_element_type=F32
            ).astype(BF)
            if padded > head_size:
                value = jnp.concatenate(
                    [value, jnp.zeros((length, padded - head_size), BF)], axis=1
                )
            attended[here, head * padded : (head + 1) * padded] = value


def attend(projected, kept, padded):
    x_count, total, wide = projected.shape
    heads = HEADS // 2
    head_size = x_count * wide // (3 * heads)
    out = jax.ShapeDtypeStruct((total, heads * padded), BF)
    vm = pl.BlockSpec(memory_space=pltpu.VMEM)
    flops = 4 * total * kept.shape[1] * heads * head_size
    return pl.pallas_call(
        lambda *refs: attend_kernel(heads, head_size, padded, *refs),
        out_shape=out,
        in_specs=[vm, vm],
        out_specs=vm,
        compiler_params=limit(projected, out),
        cost_estimate=cost(8 * flops, projected, out),
        name="attend",
    )(projected, kept)


def attend_back_kernel(heads, head_size, padded, projected, kept, upstream, out):
    group, length = kept.shape
    wide = projected.shape[2]
    scale = 1.0 / math.sqrt(head_size)

    def part(which, head, here):
        x, at = head_at(which * heads + head, head_size, wide)
        return projected[x, here, at : at + head_size]

    def put(which, head, here, value):
        x, at = head_at(which * heads + head, head_size, wide)
        out[x, here, at : at + head_size] = value.astype(BF)

    for g in range(group):
        here = pl.ds(g * length, length)
        mask = kept[g : g + 1, :]
        for head in range(heads):
            queries, keys_part, values = [part(which, head, here) for which in range(3)]
            soft = soft_of(queries, keys_part, mask)
            grads = upstream[here, head * padded : head * padded + head_size]
            grad_soft = lax.dot_general(
                grads, values, (((1,), (1,)), ((), ())), preferred_element_type=F32
            )
            total = jnp.sum(soft * grad_soft, axis=-1, keepdims=True)
            grad_scores = (soft * (grad_soft - total)).astype(BF)
            first = (((0,), (0,)), ((), ()))
            put(
                0,
                head,
                here,
                jnp.dot(grad_scores, keys_part, preferred_element_type=F32) * scale,
            )
            put(
                1,
                head,
                here,
                lax.dot_general(grad_scores, queries, first, preferred_element_type=F32) * scale,
            )
            put(
                2,
                head,
                here,
                lax.dot_general(soft.astype(BF), grads, first, preferred_element_type=F32),
            )


def attend_back(projected, kept, upstream, padded):
    x_count, total, wide = projected.shape
    heads = HEADS // 2
    head_size = x_count * wide // (3 * heads)
    out = jax.ShapeDtypeStruct(projected.shape, BF)
    vm = pl.BlockSpec(memory_space=pltpu.VMEM)
    flops = 10 * total * kept.shape[1] * heads * head_size
    return pl.pallas_call(
        lambda *refs: attend_back_kernel(heads, head_size, padded, *refs),
        out_shape=out,
        in_specs=[vm, vm, vm],
        out_specs=vm,
        compiler_params=limit(projected, upstream, out),
        cost_estimate=cost(8 * flops, projected, upstream, out),
        name="attend_back",
    )(projected, kept, upstream)

def times_plain(rows, whole, kind):
    value = jnp.einsum(
        "tr,xrk->xtk",
        jnp.moveaxis(rows, 0, 1).reshape(rows.shape[1], -1),
        whole,
        preferred_element_type=F32,
    )
    if kind == "gelu":
        return value, gelu(value).astype(BF)
    if kind == "group":
        return value.astype(BF)
    return jnp.moveaxis(value, 0, 1).reshape(value.shape[1], -1)


def by_group(grads, count):
    if len(grads.shape) == 3:
        return grads
    return jnp.moveaxis(grads.reshape(grads.shape[0], count, -1), 1, 0)


def times_back_plain(grads, whole, groups, kind, slope):
    value = jnp.einsum(
        "xtk,xrk->tr", by_group(grads, whole.shape[0]), whole, preferred_element_type=F32
    )
    value = by_group(value, groups)
    if slope is not None:
        value = value * gelu_slope(slope)
    return value.astype(kind)


def outer_plain(rows, grads, count):
    flat = jnp.moveaxis(rows, 0, 1).reshape(rows.shape[1], -1)
    return jnp.einsum(
        "tr,xtk->xrk", flat, by_group(grads, count), preferred_element_type=F32
    ).astype(BF)


def exchange(value):
    return lax.all_to_all(value, ("seq", "dp"), split_axis=0, concat_axis=0, tiled=True)


def lifted_rows(seq, dp, lifted):
    latents = lifted.shape[0]
    parts = jnp.moveaxis(lifted.reshape(latents, seq, -1), 1, 0)
    every = jnp.broadcast_to(parts[:, None], (seq, dp) + parts.shape[1:])
    return exchange(every.reshape((seq * dp,) + parts.shape[1:]))


def table_sums(seq, dp, mine, modulate):
    partial = jnp.einsum("dlr,re->dle", mine, modulate, preferred_element_type=F32)
    came = exchange(partial).reshape((seq, dp) + partial.shape[1:])
    table = jnp.moveaxis(jnp.sum(came, axis=0), 0, 1)
    table = table.reshape(table.shape[0], 6, -1)
    return [table[:, number][:, None, :] for number in range(6)]


def table_gradient(seq, dp, grad_table, mine):
    latents = grad_table.shape[0]
    parts = jnp.moveaxis(grad_table.reshape(latents, dp, -1), 1, 0)
    every = jnp.broadcast_to(parts[None], (seq,) + parts.shape)
    every = exchange(every.reshape((seq * dp,) + parts.shape[1:]))
    return jnp.einsum("dlr,dle->re", mine, every, preferred_element_type=F32)


class Block:
    def __init__(self, grid, tokens, kept_tokens, grad_out):
        self.grid, self.tokens, self.grad_out = grid, tokens, grad_out
        self.shape = tokens.shape
        self.rows = tokens.shape[0] * tokens.shape[1]
        self.kept = kept_tokens.astype(F32)
        self.mask = self.kept[:, :, None]

    def share(self, value):
        flat = value.reshape(self.rows, -1)
        return jnp.concatenate([flat, self.grid.swap(flat)])

    def settle(self, value):
        return (value[: self.rows] + self.grid.swap(value[self.rows :])).reshape(self.shape)

    def begin(self, parts):
        self.parts = parts
        shift_one, scale_one, gate_one, shift_two, scale_two, gate_two = parts
        self.grad_feed = self.share((self.mask * gate_two * self.grad_out).astype(BF))
        self.kept_both = jnp.concatenate([self.kept, self.grid.swap(self.kept)])
        self.normed_one, self.inverse_one = normalize(self.tokens)
        hidden = (self.normed_one * (1.0 + scale_one) + shift_one).astype(BF)
        self.hidden_one = self.share(hidden)[None]

    def after_attention(self, partial):
        _, _, gate_one, shift_two, scale_two, _ = self.parts
        self.attention_out = self.settle(partial)
        self.middle = self.tokens + self.mask * gate_one * self.attention_out
        self.normed_two, self.inverse_two = normalize(self.middle)
        hidden = (self.normed_two * (1.0 + scale_two) + shift_two).astype(BF)
        self.hidden_two = self.share(hidden)[None]

    def after_feed(self, partial):
        feed = self.settle(partial)
        self.result = self.middle + self.mask * self.parts[5] * feed
        self.grad_gate_two = jnp.sum(self.mask * feed * self.grad_out, axis=1)

    def back_two(self, partial):
        _, _, gate_one, _, scale_two, _ = self.parts
        grad = self.settle(partial)
        self.grad_scale_two = jnp.sum(grad * self.normed_two, axis=1)
        self.grad_shift_two = jnp.sum(grad, axis=1)
        self.grad_middle = self.grad_out + norm_back(
            grad * (1.0 + scale_two), self.normed_two, self.inverse_two
        )
        self.grad_attention = self.share((self.mask * gate_one * self.grad_middle).astype(BF))
        self.grad_gate_one = jnp.sum(self.mask * self.attention_out * self.grad_middle, axis=1)

    def back_one(self, partial):
        grad = self.settle(partial)
        self.grad_scale_one = jnp.sum(grad * self.normed_one, axis=1)
        self.grad_shift_one = jnp.sum(grad, axis=1)
        self.grad_tokens = self.grad_middle + norm_back(
            grad * (1.0 + self.parts[1]), self.normed_one, self.inverse_one
        )

    def grad_table(self):
        parts = [
            self.grad_shift_one,
            self.grad_scale_one,
            self.grad_gate_one,
            self.grad_shift_two,
            self.grad_scale_two,
            self.grad_gate_two,
        ]
        return jnp.concatenate(parts, axis=1).astype(BF)


def rounds(grid, block, lifted, modulate, entry_piece, merge_own, expand_swap, shrink_piece):
    head_size = merge_own.shape[0]
    padded = -(-head_size // 16) * 16
    merge_piece = jnp.pad(merge_own, ((0, padded - head_size), (0, 0)))
    cut = entry_piece.shape[0] // 32 * 16 + 16
    merge_row = padded // 32 * 16 + 16
    shrink_row = shrink_piece.shape[0] // 2
    dp = grid.size["x"]
    seq = 2 * grid.size["y"] * grid.size["z"]

    entry_piece, lifted = barrier((entry_piece, lifted))
    came = along_z(grid, entry_piece)
    expand_piece = expand_swap()
    mine = lifted_rows(seq, dp, lifted)
    came, expand_piece, mine, merge_piece = barrier((came, expand_piece, mine, merge_piece))
    entry_stack = jnp.stack([entry_piece] + came)

    entry_near, came = to_near(grid, entry_stack), along_z(grid, merge_piece)
    parts = table_sums(seq, dp, mine, modulate)
    entry_near, came, parts = barrier((entry_near, came, parts))
    merge_stack = jnp.stack([merge_piece] + came)

    came = along_z(grid, expand_piece)
    entry_far = to_far(grid, entry_near, cut)
    entry_far, merge_stack = barrier((entry_far, merge_stack))
    merge_near = to_near(grid, merge_stack)
    block.begin(parts)
    merge_near, block.hidden_one = barrier((merge_near, block.hidden_one))
    merge_far = to_far(grid, merge_near, merge_row)
    came, merge_far, block.hidden_one, block.grad_feed, block.kept_both = barrier(
        (came, merge_far, block.hidden_one, block.grad_feed, block.kept_both)
    )
    expand_stack = jnp.stack([expand_piece] + came)
    entry = gathered(grid, entry_stack, entry_near, entry_far, cut)
    merge = gathered(grid, merge_stack, merge_near, merge_far, merge_row)

    expand_near, came = to_near(grid, expand_stack), along_z(grid, shrink_piece)
    projected = times(block.hidden_one, entry, "group")
    attended = attend(projected, block.kept_both, padded)[None]
    partial = times(attended, merge, "columns")
    expand_near, came, partial = barrier((expand_near, came, partial))
    shrink_stack = jnp.stack([shrink_piece] + came)

    expand_far, shrink_near = to_far(grid, expand_near, cut), to_near(grid, shrink_stack)
    block.after_attention(partial)
    expand_far, shrink_near, block.hidden_two = barrier(
        (expand_far, shrink_near, block.hidden_two)
    )
    expand = gathered(grid, expand_stack, expand_near, expand_far, cut)

    shrink_far = to_far(grid, shrink_near, shrink_row)
    expanded, activated = times(block.hidden_two, expand, "gelu")
    shrink_cut = outer(grid, activated, block.grad_feed, shrink_piece.shape[0], shrink_row)
    shrink_far, shrink_cut, block.grad_feed, activated = barrier(
        (shrink_far, shrink_cut, block.grad_feed, activated)
    )
    shrink = gathered(grid, shrink_stack, shrink_near, shrink_far, shrink_row)

    shrink_first = scatter_first(grid, shrink_cut)
    grad_expanded = times_back(block.grad_feed, shrink, dp, BF, expanded)
    expand_cut = outer(grid, block.hidden_two, grad_expanded, entry_piece.shape[0], cut)
    expand_cut, grad_expanded = barrier((expand_cut, grad_expanded))
    partial = times_back(grad_expanded, expand, 1, F32)[0]
    shrink_first, expand_cut, partial, activated = barrier(
        (shrink_first, expand_cut, partial, activated)
    )

    expand_first = scatter_first(grid, expand_cut)
    block.back_two(partial)
    feed = times(activated, shrink, "columns")
    expand_first, block.grad_attention, feed = barrier(
        (expand_first, block.grad_attention, feed)
    )

    shrink_second = scatter_second(grid, shrink_cut, shrink_first)
    merge_cut = outer(grid, attended, block.grad_attention, padded, merge_row)
    grad_attended = times_back(block.grad_attention, merge, 1, BF)[0]
    grad_projected = attend_back(projected, block.kept_both, grad_attended, padded)
    shrink_second, merge_cut, grad_projected = barrier((shrink_second, merge_cut, grad_projected))

    expand_second = scatter_second(grid, expand_cut, expand_first)
    shrink_sum, shrink_z = scatter_third(grid, shrink_cut, shrink_first, shrink_second)
    entry_cut = outer(grid, block.hidden_one, grad_projected, entry_piece.shape[0], cut)
    entry_cut, grad_projected, expand_second, merge_cut = barrier(
        (entry_cut, grad_projected, expand_second, merge_cut)
    )
    merge_first = scatter_first(grid, merge_cut)
    partial = times_back(grad_projected, entry, 1, F32)[0]
    merge_first, shrink_z, partial = barrier((merge_first, shrink_z, partial))

    entry_first = scatter_first(grid, entry_cut)
    expand_sum, expand_z = scatter_third(grid, expand_cut, expand_first, expand_second)
    block.after_feed(feed)
    block.back_one(partial)
    grad_table = block.grad_table()
    shrink_sum = scatter_last(shrink_sum, shrink_z)
    entry_first, grad_table, merge_first = barrier((entry_first, grad_table, merge_first))
    merge_second = scatter_second(grid, merge_cut, merge_first)
    merge_second, expand_z, grad_table = barrier((merge_second, expand_z, grad_table))

    entry_second = scatter_second(grid, entry_cut, entry_first)
    merge_sum, merge_z = scatter_third(grid, merge_cut, merge_first, merge_second)
    modulate_sum = table_gradient(seq, dp, grad_table, mine)
    expand_sum = scatter_last(expand_sum, expand_z)
    entry_second, merge_z, modulate_sum = barrier((entry_second, merge_z, modulate_sum))

    entry_sum, entry_z = scatter_third(grid, entry_cut, entry_first, entry_second)
    merge_sum = scatter_last(merge_sum, merge_z)[:head_size]
    entry_sum = scatter_last(entry_sum, entry_z)
    return entry_sum, merge_sum, expand_sum, shrink_sum, modulate_sum


def plain(grid, block, lifted, modulate, entry_piece, merge_own, expand_swap, shrink_piece):
    dp = grid.size["x"]
    head_size = block.shape[2] // HEADS
    part_rows = merge_own.shape[0]
    seq = 2 * grid.size["y"] * grid.size["z"]
    expand_piece = expand_swap()
    mine = lifted_rows(seq, dp, lifted)
    block.begin(table_sums(seq, dp, mine, modulate))
    entry = gather_plain(grid, entry_piece)
    merge = heads_of(grid, gather_plain(grid, merge_own), part_rows, head_size)
    expand = gather_plain(grid, expand_piece)
    shrink = gather_plain(grid, shrink_piece)
    projected = times(block.hidden_one, entry, "group")
    attended = attend(projected, block.kept_both, head_size)[None]
    block.after_attention(times(attended, merge, "columns"))
    expanded, activated = times(block.hidden_two, expand, "gelu")
    block.after_feed(times(activated, shrink, "columns"))
    grad_shrink = outer_plain(activated, block.grad_feed, dp)
    grad_expanded = times_back(block.grad_feed, shrink, dp, BF, expanded)
    grad_expand = outer_plain(block.hidden_two, grad_expanded, dp)
    block.back_two(times_back(grad_expanded, expand, 1, F32)[0])
    grad_merge = outer_plain(attended, block.grad_attention, dp)
    grad_attended = times_back(block.grad_attention, merge, 1, BF)[0]
    grad_projected = attend_back(projected, block.kept_both, grad_attended, head_size)
    grad_entry = outer_plain(block.hidden_one, grad_projected, dp)
    block.back_one(times_back(grad_projected, entry, 1, F32)[0])
    modulate_sum = table_gradient(seq, dp, block.grad_table(), mine)
    return (
        scatter_plain(grid, grad_entry, 2 * part_rows),
        scatter_plain(grid, rows_of(grid, grad_merge, part_rows, head_size), part_rows),
        scatter_plain(grid, grad_expand, 2 * part_rows),
        scatter_plain(grid, grad_shrink, shrink_piece.shape[0]),
        modulate_sum,
    )


def local(seq, dp, *arguments):
    tokens, condition, kept_tokens, grad_out = arguments[:4]
    masters, velocities, averages = arguments[4:9], arguments[9:14], arguments[14:19]
    entry_own, merge_own, expand_own, shrink_own, modulate_own = [
        master.astype(BF) for master in masters
    ]
    grid = Grid(seq, dp)
    head_size = tokens.shape[2] // HEADS
    ff_block = shrink_own.shape[0]
    block = Block(grid, tokens, kept_tokens, grad_out)
    lifted = jax.nn.silu(condition).astype(BF)
    entry_mine, entry_theirs = split_core(grid, entry_own, head_size)
    expand_mine, expand_theirs = split_core(grid, expand_own, ff_block)
    entry_piece = chip_rows(grid, entry_mine, grid.swap(entry_theirs))

    def expand_swap():
        return chip_rows(grid, expand_mine, grid.swap(expand_theirs))

    whole_heads = merge_own.shape[0] == head_size
    act = rounds if dp == 2 and seq == HEADS and whole_heads else plain
    entry_sum, merge_sum, expand_sum, shrink_sum, modulate_sum = act(
        grid, block, lifted, modulate_own, entry_piece, merge_own, expand_swap, shrink_own
    )
    entry_sum = core_rows(grid, entry_sum, head_size)
    expand_sum = core_rows(grid, expand_sum, ff_block)
    summed = (entry_sum, merge_sum, expand_sum, shrink_sum, modulate_sum)
    result, grad_tokens = block.result, block.grad_tokens
    rows = block.rows

    rate = 0.03 / math.sqrt(rows * seq * dp)
    moved_list = []
    velocity_list = []
    average_list = []
    for master, velocity, average, gradient in zip(masters, velocities, averages, summed):
        fresh_velocity = DECAY * velocity + gradient
        moved = master - rate * (gradient + DECAY * fresh_velocity)
        moved_list.append(moved)
        velocity_list.append(fresh_velocity)
        average_list.append(0.5 * average + 0.5 * moved)
    return (result, grad_tokens) + tuple(moved_list) + tuple(velocity_list) + tuple(average_list)


def solution(mesh):
    spread = P(("seq", "dp"), None, None)
    flat = P(("seq", "dp"), None)
    weight = P("seq", "dp")
    seq, dp = mesh.shape["seq"], mesh.shape["dp"]
    return jax.shard_map(
        lambda *arguments: local(seq, dp, *arguments),
        mesh=mesh,
        in_specs=(spread, flat, flat, spread) + (weight,) * 15,
        out_specs=(spread, spread) + (weight,) * 15,
        check_vma=False,
    )
```

```python
import math

import jax
import jax.numpy as jnp
from jax import lax
from jax.experimental import pallas as pl
from jax.experimental.pallas import tpu as pltpu
from jax.sharding import PartitionSpec as P

HEADS = 16
EPSILON = 1e-06
DECAY = 0.5
BF = jnp.bfloat16
F32 = jnp.float32


def normalize(values):
    average = jnp.mean(values, axis=-1, keepdims=True)
    centred = values - average
    inverse = lax.rsqrt(jnp.mean(centred * centred, axis=-1, keepdims=True) + EPSILON)
    return (centred * inverse, inverse)


def norm_back(gradient, normed, inverse):
    return inverse * (
        gradient
        - jnp.mean(gradient, axis=-1, keepdims=True)
        - normed * jnp.mean(gradient * normed, axis=-1, keepdims=True)
    )


def place_kernel(count, depth, order, *refs):
    blocks, out, sems = refs[:count], refs[count], refs[count + 1]
    copies = []
    for b in range(count):
        for i in range(depth):
            at = b * depth + i
            copies.append(pltpu.make_async_copy(blocks[b].at[i], out.at[order[at]], sems.at[at]))
    for copy in copies:
        copy.start()
    for copy in copies:
        copy.wait()


def pick_kernel(count, depth, order, whole, *refs):
    blocks, sems = refs[:count], refs[count]
    copies = []
    for b in range(count):
        for i in range(depth):
            at = b * depth + i
            copies.append(pltpu.make_async_copy(whole.at[order[at]], blocks[b].at[i], sems.at[at]))
    for copy in copies:
        copy.start()
    for copy in copies:
        copy.wait()


def place(blocks, order):
    count, (depth, rows, columns) = len(blocks), blocks[0].shape
    total = count * depth
    return pl.pallas_call(
        lambda *refs: place_kernel(count, depth, *refs),
        out_shape=jax.ShapeDtypeStruct((total, rows, columns), blocks[0].dtype),
        in_specs=[pl.BlockSpec(memory_space=pltpu.SMEM)] + [pl.BlockSpec(memory_space=pl.ANY)] * count,
        out_specs=pl.BlockSpec(memory_space=pltpu.VMEM),
        scratch_shapes=[pltpu.SemaphoreType.DMA((total,))],
        compiler_params=pltpu.CompilerParams(vmem_limit_bytes=48 * 2**20),
        cost_estimate=pl.CostEstimate(
            flops=0, bytes_accessed=4 * total * rows * columns, transcendentals=0
        ),
        name="place",
    )(order, *blocks)


def pick(whole, order, count):
    total, rows, columns = whole.shape
    depth = total // count
    return pl.pallas_call(
        lambda *refs: pick_kernel(count, depth, *refs),
        out_shape=[jax.ShapeDtypeStruct((depth, rows, columns), whole.dtype)] * count,
        in_specs=[pl.BlockSpec(memory_space=pltpu.SMEM), pl.BlockSpec(memory_space=pltpu.VMEM)],
        out_specs=[pl.BlockSpec(memory_space=pl.ANY)] * count,
        scratch_shapes=[pltpu.SemaphoreType.DMA((total,))],
        compiler_params=pltpu.CompilerParams(vmem_limit_bytes=48 * 2**20),
        cost_estimate=pl.CostEstimate(
            flops=0, bytes_accessed=4 * total * rows * columns, transcendentals=0
        ),
        name="pick",
    )(order, whole)


class Grid:
    def __init__(self, seq, dp):
        self.size = {"z": 4, "y": seq // 8, "c": 2, "x": dp}
        assert seq % 8 == 0
        at, column = lax.axis_index("seq"), lax.axis_index("dp")
        sizes = self.size
        self.at = {
            "z": at // (2 * sizes["y"]),
            "y": (at // 2) % sizes["y"],
            "c": at % 2,
            "x": column,
        }

    def send(self, value, axis, shift):
        sizes = self.size
        pairs = []
        for z in range(sizes["z"]):
            for y in range(sizes["y"]):
                for c in range(2):
                    for x in range(sizes["x"]):
                        here = {"z": z, "y": y, "c": c, "x": x}
                        there = dict(here)
                        there[axis] = (here[axis] + shift) % sizes[axis]
                        pairs.append((self.flat(here), self.flat(there)))
        return lax.ppermute(value, ("seq", "dp"), pairs)

    def flat(self, p):
        sizes = self.size
        return ((p["z"] * sizes["y"] + p["y"]) * 2 + p["c"]) * sizes["x"] + p["x"]

    def swap(self, value):
        return self.send(value, "c", 1)

    def off(self, axis, shift):
        return (self.at[axis] + shift) % self.size[axis]


barrier = lax.optimization_barrier


def gather_plain(grid, piece):
    sizes = grid.size
    stack = jnp.stack([piece] + [grid.send(piece, "z", shift) for shift in range(1, sizes["z"])])
    line = [stack] + [grid.send(stack, "y", shift) for shift in range(1, sizes["y"])]
    whole = lax.all_gather(jnp.stack(line), "dp", axis=0)
    blocks = [whole[x, sy] for x in range(sizes["x"]) for sy in range(sizes["y"])]
    order = plain_order(grid, -1)
    return place(blocks, order).reshape(sizes["x"], -1, piece.shape[1])


def scatter_plain(grid, whole, rows):
    sizes = grid.size
    count = sizes["x"] * sizes["y"]
    blocks = pick(whole.reshape(-1, rows, whole.shape[-1]), plain_order(grid, 1), count)
    pairs = jnp.stack(blocks).reshape((sizes["x"], sizes["y"]) + blocks[0].shape)
    kept = lax.psum_scatter(pairs, "dp", scatter_dimension=0).astype(F32)
    total = kept[0]
    for near in range(1, sizes["y"]):
        total = total + grid.send(kept[near].astype(BF), "y", near).astype(F32)
    return scatter_z(grid, total)


def scatter_z(grid, total):
    result = total[0]
    for shift in range(1, grid.size["z"]):
        result = result + grid.send(total[shift].astype(BF), "z", shift).astype(F32)
    return result


def plain_order(grid, sign):
    sizes = grid.size
    result = []
    for x in range(sizes["x"]):
        for sy in range(sizes["y"]):
            for sz in range(sizes["z"]):
                y, z = grid.off("y", sign * sy), grid.off("z", sign * sz)
                result.append((x * sizes["z"] + z) * sizes["y"] + y)
    return jnp.stack(result).astype(jnp.int32)


def along_z(grid, piece):
    return [grid.send(piece, "z", shift) for shift in range(1, grid.size["z"])]


def to_near(grid, stack):
    return [grid.send(stack, axis, 1) for axis in "xy"]


def to_far(grid, near, cut):
    by_x, by_y = near
    return [grid.send(by_y[:, :cut], "x", 1), grid.send(by_x[:, cut:], "y", 1)]


def gathered(grid, stack, near, far, cut):
    blocks = [(stack, 0, 0, 0), (near[1], 0, 1, 0), (near[0], 1, 0, 0)]
    return Weight(grid, blocks + [(far[0], 1, 1, 0), (far[1], 1, 1, cut)])


def scatter_first(grid, blocks):
    _, away_x, _, away_y = blocks
    return [grid.send(away_x, "x", 1), grid.send(away_y, "y", 1)]


def scatter_second(grid, blocks, came):
    kept_x, _, kept_y, _ = blocks
    by_x = (kept_x[1].astype(F32) + came[0][1].astype(F32)).astype(BF)
    by_y = (kept_y[1].astype(F32) + came[1][1].astype(F32)).astype(BF)
    return [grid.send(by_x, "y", 1), grid.send(by_y, "x", 1)]


def scatter_third(blocks, came, more):
    parts = [
        kept[0].astype(F32) + near[0].astype(F32) + far.astype(F32)
        for kept, near, far in zip(blocks[::2], came, more)
    ]
    total = jnp.concatenate(parts, axis=1)
    return total[0], total[1:].astype(BF)


def scatter_last(own, came):
    for value in came:
        own = own + value.astype(F32)
    return own


def heads_of(grid, whole, rows, head_size):
    if rows % head_size == 0:
        return whole
    assert head_size == 2 * rows
    first = grid.at["c"] == 0
    halves = whole.reshape(whole.shape[0], HEADS // 2, 2, rows, -1)
    even, odd = halves[:, :, 0], halves[:, :, 1]
    kept = jnp.where(first, even, odd)
    came = grid.swap(jnp.where(first, odd, even))
    low, high = jnp.where(first, kept, came), jnp.where(first, came, kept)
    return jnp.stack([low, high], axis=2).reshape(whole.shape)


def rows_of(grid, whole, rows, head_size):
    if rows % head_size == 0:
        return whole
    first = grid.at["c"] == 0
    halves = whole.reshape(whole.shape[0], HEADS // 2, 2, rows, -1)
    low, high = halves[:, :, 0], halves[:, :, 1]
    kept = jnp.where(first, low, high)
    came = grid.swap(jnp.where(first, high, low))
    even, odd = jnp.where(first, kept, came), jnp.where(first, came, kept)
    return jnp.stack([even, odd], axis=2).reshape(whole.shape)


def split_core(grid, weight, block):
    rows, columns = weight.shape
    pairs = weight.reshape(rows, columns // (2 * block), 2, block)
    even = pairs[:, :, 0].reshape(rows, -1)
    odd = pairs[:, :, 1].reshape(rows, -1)
    first = grid.at["c"] == 0
    return (jnp.where(first, even, odd), jnp.where(first, odd, even))


def join_core(grid, own, other, block):
    rows, columns = own.shape
    first = grid.at["c"] == 0
    even = jnp.where(first, own, other).reshape(rows, -1, 1, block)
    odd = jnp.where(first, other, own).reshape(rows, -1, 1, block)
    return jnp.concatenate([even, odd], axis=2).reshape(rows, 2 * columns)


def chip_rows(grid, own, other):
    first = grid.at["c"] == 0
    return jnp.concatenate([jnp.where(first, own, other), jnp.where(first, other, own)])


def core_rows(grid, summed, block):
    rows = summed.shape[0] // 2
    first = grid.at["c"] == 0
    low, high = summed[:rows], summed[rows:]
    own = jnp.where(first, low, high)
    other = grid.swap(jnp.where(first, high, low))
    return join_core(grid, own, other, block)


GELU_A = 0.7978845608028654
GELU_B = 0.044715


def gelu(v):
    return 0.5 * v * (1.0 + jnp.tanh(GELU_A * (v + GELU_B * (v * v * v))))


def gelu_slope(v):
    inner = jnp.tanh(GELU_A * (v + GELU_B * (v * v * v)))
    return 0.5 * (1.0 + inner) + 0.5 * v * (1.0 - inner * inner) * (
        GELU_A * (1.0 + 3.0 * GELU_B * v * v)
    )


class Weight:
    def __init__(self, grid, blocks):
        self.grid = grid
        self.order = place_of(grid, -1)
        self.blocks = [block[0] for block in blocks]
        self.marks = [block[1:] for block in blocks]
        _, self.tall, wide = self.blocks[0].shape
        sizes = grid.size
        self.shape = (sizes["x"], sizes["z"] * sizes["y"] * self.tall, wide)


def place_of(grid, sign):
    sizes = grid.size
    result = []
    for axis in "xyz":
        result += [grid.off(axis, sign * shift) for shift in range(sizes[axis])]
    return jnp.stack(result).astype(jnp.int32)


def spot(whole, order, mark, sz, tall, rows):
    sx, sy, offset = mark
    x, y, z = order[sx], order[2 + sy], order[4 + sz]
    return whole.at[x, pl.ds(pl.multiple_of((z * 2 + y) * tall + offset, 16), rows), :]


def fill(blocks, order, whole, tall, marks):
    for block, mark in zip(blocks, marks):
        depth, rows, _ = block.shape

        def put(i, carry, block=block, mark=mark, rows=rows):
            spot(whole, order, mark, i, tall, rows)[...] = block[i]
            return carry

        lax.fori_loop(0, depth, put, 0)


def cost(flops, *arrays):
    return pl.CostEstimate(flops=1024, bytes_accessed=1024, transcendentals=0)


def limit(*arrays):
    total = sum(math.prod(a.shape) * jnp.dtype(a.dtype).itemsize for a in arrays)
    return pltpu.CompilerParams(vmem_limit_bytes=min(56 * 2**20, total * 9 // 8 + 16 * 2**20))


STEP = 256


def times_kernel(count, tall, marks, finish, order, rows, *refs):
    blocks, outs, whole = refs[:count], refs[count:-1], refs[-1]
    fill(blocks, order, whole, tall, marks)
    groups, total, depth = rows.shape
    for x in range(whole.shape[0]):
        for start in range(0, total, STEP):
            here = pl.ds(start, STEP)
            value = None
            for a in range(groups):
                part = jnp.dot(
                    rows[a, here, :],
                    whole[x, a * depth : (a + 1) * depth, :],
                    preferred_element_type=F32,
                )
                value = part if value is None else value + part
            finish(x, here, value, outs)


def to_group(x, here, value, outs):
    outs[0][x, here, :] = value.astype(outs[0].dtype)


def to_columns(x, here, value, outs):
    wide = value.shape[1]
    outs[0][here, x * wide : (x + 1) * wide] = value.astype(outs[0].dtype)


def to_gelu(x, here, value, outs):
    outs[0][x, here, :] = value
    outs[1][x, here, :] = gelu(value).astype(BF)


def fused(kernel, name, weight, flops, outs, before, after=()):
    blocks = weight.blocks
    whole = jax.ShapeDtypeStruct(weight.shape, BF)
    vm = pl.BlockSpec(memory_space=pltpu.VMEM)
    return pl.pallas_call(
        lambda *refs: kernel(len(blocks), weight.tall, weight.marks, *refs),
        out_shape=outs,
        in_specs=[pl.BlockSpec(memory_space=pltpu.SMEM)]
        + [vm] * (len(before) + len(blocks) + len(after)),
        out_specs=[vm] * len(outs),
        scratch_shapes=[pltpu.VMEM(weight.shape, BF)],
        compiler_params=limit(whole, whole, *before, *after, *outs),
        cost_estimate=cost(flops, whole, *before, *after, *outs),
        name=name,
    )(weight.order, *before, *blocks, *after)


def times(rows, weight, kind):
    if not isinstance(weight, Weight):
        return times_plain(rows, weight, kind)
    groups, total, depth = rows.shape
    x_count, tall, wide = weight.shape
    flops = 2 * total * tall * wide * x_count
    if kind == "gelu":
        finish = to_gelu
        outs = [
            jax.ShapeDtypeStruct((x_count, total, wide), F32),
            jax.ShapeDtypeStruct((x_count, total, wide), BF),
        ]
    elif kind == "group":
        finish, outs = to_group, [jax.ShapeDtypeStruct((x_count, total, wide), BF)]
    else:
        finish, outs = to_columns, [jax.ShapeDtypeStruct((total, x_count * wide), F32)]

    def kernel(count, tall, marks, *refs):
        times_kernel(count, tall, marks, finish, *refs)

    result = fused(kernel, "times", weight, flops, outs, (rows,))
    return result if len(result) > 1 else result[0]


def back_kernel(count, tall, marks, order, grads, *refs):
    blocks = refs[:count]
    whole, rest = refs[-1], refs[count:-1]
    out, slope = rest[-1], (rest[0] if len(rest) > 1 else None)
    fill(blocks, order, whole, tall, marks)
    x_count, depth, wide = whole.shape
    groups, total, part = out.shape
    for a in range(groups):
        for start in range(0, total, STEP):
            here = pl.ds(start, STEP)
            value = None
            for x in range(x_count):
                if len(grads.shape) == 3:
                    left = grads[x, here, :]
                else:
                    left = grads[here, x * wide : (x + 1) * wide]
                term = lax.dot_general(
                    left,
                    whole[x, a * part : (a + 1) * part, :],
                    (((1,), (1,)), ((), ())),
                    preferred_element_type=F32,
                )
                value = term if value is None else value + term
            if slope is not None:
                value = value * gelu_slope(slope[a, here, :])
            out[a, here, :] = value.astype(out.dtype)


def times_back(grads, weight, groups, kind, slope=None):
    if not isinstance(weight, Weight):
        return times_back_plain(grads, weight, groups, kind, slope)
    x_count, tall, wide = weight.shape
    total = grads.shape[-2]
    flops = 2 * total * tall * wide * x_count
    outs = [jax.ShapeDtypeStruct((groups, total, tall // groups), kind)]
    after = () if slope is None else (slope,)
    return fused(back_kernel, "times_back", weight, flops, outs, (grads,), after)[0]


def outer_kernel(tall, marks, order, rows, grads, *refs):
    blocks, whole, sems = refs[:-2], refs[-2], refs[-1]
    groups, _, depth = rows.shape
    x_count, _, wide = whole.shape
    for x in range(x_count):
        right = grads[x, :, :] if len(grads.shape) == 3 else grads[:, x * wide : (x + 1) * wide]
        for a in range(groups):
            value = lax.dot_general(
                rows[a, :, :], right, (((0,), (0,)), ((), ())), preferred_element_type=F32
            )
            whole[x, a * depth : (a + 1) * depth, :] = value.astype(BF)
    copies = []
    for block, pair in zip(blocks, marks):
        _, deep, high, _ = block.shape
        for j, mark in enumerate(pair):
            for i in range(deep):
                there = spot(whole, order, mark, i, tall, high)
                sem = sems.at[len(copies)]
                copies.append(pltpu.make_async_copy(there, block.at[j, i], sem))
    for copy in copies:
        copy.start()
    for copy in copies:
        copy.wait()


def outer(grid, rows, grads, tall, cut):
    sizes = grid.size
    groups, total, depth = rows.shape
    x_count = sizes["x"]
    wide = grads.shape[-1] if len(grads.shape) == 3 else grads.shape[1] // x_count
    outs, marks = [], []
    for start, high, by_x in ((0, cut, True), (cut, tall - cut, False)):
        for away in (0, 1):
            if high:
                outs.append(jax.ShapeDtypeStruct((2, sizes["z"], high, wide), BF))
                marks.append(
                    [(away, j, start) if by_x else (j, away, start) for j in range(2)]
                )
    assert groups * depth == sizes["z"] * sizes["y"] * tall
    whole = jax.ShapeDtypeStruct((x_count, groups * depth, wide), BF)
    vm = pl.BlockSpec(memory_space=pltpu.VMEM)
    flops = 2 * total * groups * depth * wide * x_count
    blocks = pl.pallas_call(
        lambda *refs: outer_kernel(tall, marks, *refs),
        out_shape=outs,
        in_specs=[pl.BlockSpec(memory_space=pltpu.SMEM), vm, vm],
        out_specs=[pl.BlockSpec(memory_space=pl.ANY)] * len(outs),
        scratch_shapes=[
            pltpu.VMEM(whole.shape, BF),
            pltpu.SemaphoreType.DMA((len(outs) * 2 * sizes["z"],)),
        ],
        compiler_params=limit(whole, rows, grads),
        cost_estimate=cost(flops, whole, rows, grads),
        name="outer",
    )(place_of(grid, 1), rows, grads)
    return tuple(blocks) + (None,) * (4 - len(blocks))


def head_at(number, head_size, wide):
    start = number * head_size
    return start // wide, start % wide


def soft_of(queries, keys_part, kept):
    scale = 1.0 / math.sqrt(queries.shape[1])
    scores = lax.dot_general(
        queries, keys_part, (((1,), (1,)), ((), ())), preferred_element_type=F32
    )
    scores = jnp.where(kept > 0, scores * scale, -1000000000.0)
    exponent = jnp.exp(scores - jnp.max(scores, axis=-1, keepdims=True))
    return exponent * (1.0 / jnp.sum(exponent, axis=-1, keepdims=True))


def attend_kernel(heads, head_size, padded, projected, kept, attended):
    group, length = kept.shape
    wide = projected.shape[2]

    def part(which, head, here):
        x, at = head_at(which * heads + head, head_size, wide)
        return projected[x, here, at : at + head_size]

    for g in range(group):
        here = pl.ds(g * length, length)
        mask = kept[g : g + 1, :]
        for head in range(heads):
            soft = soft_of(part(0, head, here), part(1, head, here), mask)
            value = jnp.dot(
                soft.astype(BF), part(2, head, here), preferred_element_type=F32
            ).astype(BF)
            if padded > head_size:
                value = jnp.concatenate(
                    [value, jnp.zeros((length, padded - head_size), BF)], axis=1
                )
            attended[here, head * padded : (head + 1) * padded] = value


def attend(projected, kept, padded):
    x_count, total, wide = projected.shape
    heads = HEADS // 2
    head_size = x_count * wide // (3 * heads)
    out = jax.ShapeDtypeStruct((total, heads * padded), BF)
    vm = pl.BlockSpec(memory_space=pltpu.VMEM)
    flops = 4 * total * kept.shape[1] * heads * head_size
    return pl.pallas_call(
        lambda *refs: attend_kernel(heads, head_size, padded, *refs),
        out_shape=out,
        in_specs=[vm, vm],
        out_specs=vm,
        compiler_params=limit(projected, out),
        cost_estimate=cost(8 * flops, projected, out),
        name="attend",
    )(projected, kept)


def attend_back_kernel(heads, head_size, padded, projected, kept, upstream, out):
    group, length = kept.shape
    wide = projected.shape[2]
    scale = 1.0 / math.sqrt(head_size)

    def part(which, head, here):
        x, at = head_at(which * heads + head, head_size, wide)
        return projected[x, here, at : at + head_size]

    def put(which, head, here, value):
        x, at = head_at(which * heads + head, head_size, wide)
        out[x, here, at : at + head_size] = value.astype(BF)

    for g in range(group):
        here = pl.ds(g * length, length)
        mask = kept[g : g + 1, :]
        for head in range(heads):
            queries, keys_part, values = [part(which, head, here) for which in range(3)]
            soft = soft_of(queries, keys_part, mask)
            grads = upstream[here, head * padded : head * padded + head_size]
            grad_soft = lax.dot_general(
                grads, values, (((1,), (1,)), ((), ())), preferred_element_type=F32
            )
            total = jnp.sum(soft * grad_soft, axis=-1, keepdims=True)
            grad_scores = (soft * (grad_soft - total)).astype(BF)
            first = (((0,), (0,)), ((), ()))
            put(
                0,
                head,
                here,
                jnp.dot(grad_scores, keys_part, preferred_element_type=F32) * scale,
            )
            put(
                1,
                head,
                here,
                lax.dot_general(grad_scores, queries, first, preferred_element_type=F32) * scale,
            )
            put(
                2,
                head,
                here,
                lax.dot_general(soft.astype(BF), grads, first, preferred_element_type=F32),
            )


def attend_back(projected, kept, upstream, padded):
    x_count, total, wide = projected.shape
    heads = HEADS // 2
    head_size = x_count * wide // (3 * heads)
    out = jax.ShapeDtypeStruct(projected.shape, BF)
    vm = pl.BlockSpec(memory_space=pltpu.VMEM)
    flops = 10 * total * kept.shape[1] * heads * head_size
    return pl.pallas_call(
        lambda *refs: attend_back_kernel(heads, head_size, padded, *refs),
        out_shape=out,
        in_specs=[vm, vm, vm],
        out_specs=vm,
        compiler_params=limit(projected, upstream, out),
        cost_estimate=cost(8 * flops, projected, upstream, out),
        name="attend_back",
    )(projected, kept, upstream)

def times_plain(rows, whole, kind):
    value = jnp.einsum(
        "tr,xrk->xtk",
        jnp.moveaxis(rows, 0, 1).reshape(rows.shape[1], -1),
        whole,
        preferred_element_type=F32,
    )
    if kind == "gelu":
        return value, gelu(value).astype(BF)
    if kind == "group":
        return value.astype(BF)
    return jnp.moveaxis(value, 0, 1).reshape(value.shape[1], -1)


def by_group(grads, count):
    if len(grads.shape) == 3:
        return grads
    return jnp.moveaxis(grads.reshape(grads.shape[0], count, -1), 1, 0)


def times_back_plain(grads, whole, groups, kind, slope):
    value = jnp.einsum(
        "xtk,xrk->tr", by_group(grads, whole.shape[0]), whole, preferred_element_type=F32
    )
    value = by_group(value, groups)
    if slope is not None:
        value = value * gelu_slope(slope)
    return value.astype(kind)


def outer_plain(rows, grads, count):
    flat = jnp.moveaxis(rows, 0, 1).reshape(rows.shape[1], -1)
    return jnp.einsum(
        "tr,xtk->xrk", flat, by_group(grads, count), preferred_element_type=F32
    ).astype(BF)


def exchange(value):
    return lax.all_to_all(value, ("seq", "dp"), split_axis=0, concat_axis=0, tiled=True)


def lifted_rows(seq, dp, lifted):
    latents = lifted.shape[0]
    parts = jnp.moveaxis(lifted.reshape(latents, seq, -1), 1, 0)
    every = jnp.broadcast_to(parts[:, None], (seq, dp) + parts.shape[1:])
    return exchange(every.reshape((seq * dp,) + parts.shape[1:]))


def table_sums(seq, dp, mine, modulate):
    partial = jnp.einsum("dlr,re->dle", mine, modulate, preferred_element_type=F32)
    came = exchange(partial).reshape((seq, dp) + partial.shape[1:])
    table = jnp.moveaxis(jnp.sum(came, axis=0), 0, 1)
    table = table.reshape(table.shape[0], 6, -1)
    return [table[:, number][:, None, :] for number in range(6)]


def table_gradient(seq, dp, grad_table, mine):
    latents = grad_table.shape[0]
    parts = jnp.moveaxis(grad_table.reshape(latents, dp, -1), 1, 0)
    every = jnp.broadcast_to(parts[None], (seq,) + parts.shape)
    every = exchange(every.reshape((seq * dp,) + parts.shape[1:]))
    return jnp.einsum("dlr,dle->re", mine, every, preferred_element_type=F32)


class Block:
    def __init__(self, grid, tokens, kept_tokens, grad_out):
        self.grid, self.tokens, self.grad_out = grid, tokens, grad_out
        self.shape = tokens.shape
        self.rows = tokens.shape[0] * tokens.shape[1]
        self.kept = kept_tokens.astype(F32)
        self.mask = self.kept[:, :, None]

    def share(self, value):
        flat = value.reshape(self.rows, -1)
        return jnp.concatenate([flat, self.grid.swap(flat)])

    def settle(self, value):
        return (value[: self.rows] + self.grid.swap(value[self.rows :])).reshape(self.shape)

    def begin(self, parts):
        self.parts = parts
        shift_one, scale_one, gate_one, shift_two, scale_two, gate_two = parts
        self.grad_feed = self.share((self.mask * gate_two * self.grad_out).astype(BF))
        self.kept_both = jnp.concatenate([self.kept, self.grid.swap(self.kept)])
        self.normed_one, self.inverse_one = normalize(self.tokens)
        self.hidden_one = (self.normed_one * (1.0 + scale_one) + shift_one).astype(BF)

    def after_attention(self, partial):
        _, _, gate_one, shift_two, scale_two, _ = self.parts
        self.attention_out = self.settle(partial)
        self.middle = self.tokens + self.mask * gate_one * self.attention_out
        self.normed_two, self.inverse_two = normalize(self.middle)
        hidden = (self.normed_two * (1.0 + scale_two) + shift_two).astype(BF)
        self.hidden_two = self.share(hidden)[None]

    def after_feed(self, partial):
        feed = self.settle(partial)
        self.result = self.middle + self.mask * self.parts[5] * feed
        self.grad_gate_two = jnp.sum(self.mask * feed * self.grad_out, axis=1)

    def back_two(self, partial):
        _, _, gate_one, _, scale_two, _ = self.parts
        grad = self.settle(partial)
        self.grad_scale_two = jnp.sum(grad * self.normed_two, axis=1)
        self.grad_shift_two = jnp.sum(grad, axis=1)
        self.grad_middle = self.grad_out + norm_back(
            grad * (1.0 + scale_two), self.normed_two, self.inverse_two
        )
        self.grad_attention = self.share((self.mask * gate_one * self.grad_middle).astype(BF))
        self.grad_gate_one = jnp.sum(self.mask * self.attention_out * self.grad_middle, axis=1)

    def back_one(self, partial):
        grad = self.settle(partial)
        self.grad_scale_one = jnp.sum(grad * self.normed_one, axis=1)
        self.grad_shift_one = jnp.sum(grad, axis=1)
        self.grad_tokens = self.grad_middle + norm_back(
            grad * (1.0 + self.parts[1]), self.normed_one, self.inverse_one
        )

    def grad_table(self):
        parts = [
            self.grad_shift_one,
            self.grad_scale_one,
            self.grad_gate_one,
            self.grad_shift_two,
            self.grad_scale_two,
            self.grad_gate_two,
        ]
        return jnp.concatenate(parts, axis=1).astype(BF)


def rounds(grid, block, lifted, modulate, entry_piece, merge_own, expand_swap, shrink_piece):
    head_size = merge_own.shape[0]
    padded = -(-head_size // 16) * 16
    merge_piece = jnp.pad(merge_own, ((0, padded - head_size), (0, 0)))
    cut = entry_piece.shape[0] // 32 * 16 + 16
    merge_row = padded // 32 * 16 + 16
    shrink_row = shrink_piece.shape[0] // 2
    dp = grid.size["x"]
    seq = 2 * grid.size["y"] * grid.size["z"]

    entry_piece, lifted = barrier((entry_piece, lifted))
    came = along_z(grid, entry_piece), along_z(grid, merge_piece)
    expand_piece = expand_swap()
    mine = lifted_rows(seq, dp, lifted)
    came, expand_piece, mine = barrier((came, expand_piece, mine))
    entry_stack = jnp.stack([entry_piece] + came[0])
    merge_stack = jnp.stack([merge_piece] + came[1])

    entry_near, merge_near = to_near(grid, entry_stack), to_near(grid, merge_stack)
    two = grid.send(expand_piece, "z", 2)
    parts = table_sums(seq, dp, mine, modulate)
    entry_near, merge_near, two, parts, expand_piece = barrier(
        (entry_near, merge_near, two, parts, expand_piece)
    )

    entry_far, merge_far = to_far(grid, entry_near, cut), to_far(grid, merge_near, merge_row)
    one, three = grid.send(expand_piece, "z", 1), grid.send(expand_piece, "z", 3)
    block.begin(parts)
    block.hidden_one = block.share(block.hidden_one)[None]
    entry_far, merge_far, one, three, block.hidden_one = barrier(
        (entry_far, merge_far, one, three, block.hidden_one)
    )
    expand_stack = jnp.stack([expand_piece, one, two, three])
    entry = gathered(grid, entry_stack, entry_near, entry_far, cut)
    merge = gathered(grid, merge_stack, merge_near, merge_far, merge_row)

    expand_near, came = to_near(grid, expand_stack), along_z(grid, shrink_piece)
    projected = times(block.hidden_one, entry, "group")
    attended = attend(projected, block.kept_both, padded)[None]
    partial = times(attended, merge, "columns")
    expand_near, came, partial = barrier((expand_near, came, partial))
    shrink_stack = jnp.stack([shrink_piece] + came)

    expand_far = to_far(grid, expand_near, cut)
    block.after_attention(partial)
    expand_far, block.hidden_two, shrink_stack = barrier(
        (expand_far, block.hidden_two, shrink_stack)
    )

    shrink_near = to_near(grid, shrink_stack)
    expand = gathered(grid, expand_stack, expand_near, expand_far, cut)
    expanded, activated = times(block.hidden_two, expand, "gelu")
    grad_feed = block.grad_feed
    shrink_cut = outer(grid, activated, grad_feed, shrink_piece.shape[0], shrink_row)
    shrink_near, shrink_cut, grad_feed, activated = barrier(
        (shrink_near, shrink_cut, grad_feed, activated)
    )

    shrink_far = to_far(grid, shrink_near, shrink_row)
    shrink_far, grad_feed, shrink_cut = barrier((shrink_far, grad_feed, shrink_cut))

    shrink_first = scatter_first(grid, shrink_cut)
    shrink = gathered(grid, shrink_stack, shrink_near, shrink_far, shrink_row)
    grad_expanded = times_back(grad_feed, shrink, dp, BF, expanded)
    expand_cut = outer(grid, block.hidden_two, grad_expanded, entry_piece.shape[0], cut)
    expand_cut, grad_expanded = barrier((expand_cut, grad_expanded))
    partial = times_back(grad_expanded, expand, 1, F32)[0]
    shrink_first, expand_cut, partial, activated = barrier(
        (shrink_first, expand_cut, partial, activated)
    )

    expand_first = scatter_first(grid, expand_cut)
    block.back_two(partial)
    feed = times(activated, shrink, "columns")
    expand_first, block.grad_attention, feed = barrier(
        (expand_first, block.grad_attention, feed)
    )

    shrink_second = scatter_second(grid, shrink_cut, shrink_first)
    merge_cut = outer(grid, attended, block.grad_attention, padded, merge_row)
    merge_cut, grad_attention = barrier((merge_cut, block.grad_attention))
    merge_first = scatter_first(grid, merge_cut)
    grad_attended = times_back(grad_attention, merge, 1, BF)[0]
    grad_projected = attend_back(projected, block.kept_both, grad_attended, padded)
    shrink_second, merge_first, grad_projected = barrier(
        (shrink_second, merge_first, grad_projected)
    )

    expand_second = scatter_second(grid, expand_cut, expand_first)
    shrink_sum, shrink_low = scatter_third(shrink_cut, shrink_first, shrink_second)
    shrink_z = [grid.send(shrink_low[i], "z", i + 1) for i in range(3)]
    entry_cut = outer(grid, block.hidden_one, grad_projected, entry_piece.shape[0], cut)
    partial = times_back(grad_projected, entry, 1, F32)[0]
    expand_second, shrink_z, entry_cut, partial = barrier(
        (expand_second, shrink_z, entry_cut, partial)
    )

    entry_first = scatter_first(grid, entry_cut)
    merge_second = scatter_second(grid, merge_cut, merge_first)
    expand_sum, expand_low = scatter_third(expand_cut, expand_first, expand_second)
    expand_z = [grid.send(expand_low[0], "z", 1)]
    block.after_feed(feed)
    block.back_one(partial)
    grad_table = block.grad_table()
    shrink_sum = scatter_last(shrink_sum, shrink_z)
    entry_first, merge_second, expand_z, grad_table = barrier(
        (entry_first, merge_second, expand_z, grad_table)
    )

    entry_second = scatter_second(grid, entry_cut, entry_first)
    merge_sum, merge_low = scatter_third(merge_cut, merge_first, merge_second)
    expand_z += [grid.send(expand_low[i], "z", i + 1) for i in (1, 2)]
    merge_z = [grid.send(merge_low[0], "z", 1)]
    entry_second, expand_z, merge_z, grad_table = barrier(
        (entry_second, expand_z, merge_z, grad_table)
    )

    entry_sum, entry_low = scatter_third(entry_cut, entry_first, entry_second)
    entry_z = [grid.send(entry_low[i], "z", i + 1) for i in range(3)]
    modulate_sum = table_gradient(seq, dp, grad_table, mine)
    merge_z += [grid.send(merge_low[i], "z", i + 1) for i in (1, 2)]
    expand_sum = scatter_last(expand_sum, expand_z)
    entry_z, modulate_sum = barrier((entry_z, modulate_sum))
    merge_sum = scatter_last(merge_sum, merge_z)[:head_size]
    entry_sum = scatter_last(entry_sum, entry_z)
    return entry_sum, merge_sum, expand_sum, shrink_sum, modulate_sum


def plain(grid, block, lifted, modulate, entry_piece, merge_own, expand_swap, shrink_piece):
    dp = grid.size["x"]
    head_size = block.shape[2] // HEADS
    part_rows = merge_own.shape[0]
    seq = 2 * grid.size["y"] * grid.size["z"]
    expand_piece = expand_swap()
    mine = lifted_rows(seq, dp, lifted)
    block.begin(table_sums(seq, dp, mine, modulate))
    block.hidden_one = block.share(block.hidden_one)[None]
    entry = gather_plain(grid, entry_piece)
    merge = heads_of(grid, gather_plain(grid, merge_own), part_rows, head_size)
    expand = gather_plain(grid, expand_piece)
    shrink = gather_plain(grid, shrink_piece)
    projected = times(block.hidden_one, entry, "group")
    attended = attend(projected, block.kept_both, head_size)[None]
    block.after_attention(times(attended, merge, "columns"))
    expanded, activated = times(block.hidden_two, expand, "gelu")
    block.after_feed(times(activated, shrink, "columns"))
    grad_shrink = outer_plain(activated, block.grad_feed, dp)
    grad_expanded = times_back(block.grad_feed, shrink, dp, BF, expanded)
    grad_expand = outer_plain(block.hidden_two, grad_expanded, dp)
    block.back_two(times_back(grad_expanded, expand, 1, F32)[0])
    grad_merge = outer_plain(attended, block.grad_attention, dp)
    grad_attended = times_back(block.grad_attention, merge, 1, BF)[0]
    grad_projected = attend_back(projected, block.kept_both, grad_attended, head_size)
    grad_entry = outer_plain(block.hidden_one, grad_projected, dp)
    block.back_one(times_back(grad_projected, entry, 1, F32)[0])
    modulate_sum = table_gradient(seq, dp, block.grad_table(), mine)
    return (
        scatter_plain(grid, grad_entry, 2 * part_rows),
        scatter_plain(grid, rows_of(grid, grad_merge, part_rows, head_size), part_rows),
        scatter_plain(grid, grad_expand, 2 * part_rows),
        scatter_plain(grid, grad_shrink, shrink_piece.shape[0]),
        modulate_sum,
    )


def local(seq, dp, *arguments):
    tokens, condition, kept_tokens, grad_out = arguments[:4]
    masters, velocities, averages = arguments[4:9], arguments[9:14], arguments[14:19]
    entry_own, merge_own, expand_own, shrink_own, modulate_own = [
        master.astype(BF) for master in masters
    ]
    grid = Grid(seq, dp)
    head_size = tokens.shape[2] // HEADS
    ff_block = shrink_own.shape[0]
    block = Block(grid, tokens, kept_tokens, grad_out)
    lifted = jax.nn.silu(condition).astype(BF)
    entry_mine, entry_theirs = split_core(grid, entry_own, head_size)
    expand_mine, expand_theirs = split_core(grid, expand_own, ff_block)
    entry_piece = chip_rows(grid, entry_mine, grid.swap(entry_theirs))

    def expand_swap():
        return chip_rows(grid, expand_mine, grid.swap(expand_theirs))

    whole_heads = merge_own.shape[0] == head_size
    act = rounds if dp == 2 and seq == HEADS and whole_heads else plain
    entry_sum, merge_sum, expand_sum, shrink_sum, modulate_sum = act(
        grid, block, lifted, modulate_own, entry_piece, merge_own, expand_swap, shrink_own
    )
    entry_sum = core_rows(grid, entry_sum, head_size)
    expand_sum = core_rows(grid, expand_sum, ff_block)
    summed = (entry_sum, merge_sum, expand_sum, shrink_sum, modulate_sum)
    result, grad_tokens = block.result, block.grad_tokens
    rows = block.rows

    rate = 0.03 / math.sqrt(rows * seq * dp)
    moved_list = []
    velocity_list = []
    average_list = []
    for master, velocity, average, gradient in zip(masters, velocities, averages, summed):
        fresh_velocity = DECAY * velocity + gradient
        moved = master - rate * (gradient + DECAY * fresh_velocity)
        moved_list.append(moved)
        velocity_list.append(fresh_velocity)
        average_list.append(0.5 * average + 0.5 * moved)
    return (result, grad_tokens) + tuple(moved_list) + tuple(velocity_list) + tuple(average_list)


def solution(mesh):
    spread = P(("seq", "dp"), None, None)
    flat = P(("seq", "dp"), None)
    weight = P("seq", "dp")
    seq, dp = mesh.shape["seq"], mesh.shape["dp"]
    return jax.shard_map(
        lambda *arguments: local(seq, dp, *arguments),
        mesh=mesh,
        in_specs=(spread, flat, flat, spread) + (weight,) * 15,
        out_specs=(spread, spread) + (weight,) * 15,
        check_vma=False,
    )
```

```python
import math

import jax
import jax.numpy as jnp
from jax import lax
from jax.experimental import pallas as pl
from jax.experimental.pallas import tpu as pltpu
from jax.sharding import PartitionSpec as P

HEADS = 16
EPSILON = 1e-06
DECAY = 0.5
BF = jnp.bfloat16
F32 = jnp.float32


def normalize(values):
    average = jnp.mean(values, axis=-1, keepdims=True)
    centred = values - average
    inverse = lax.rsqrt(jnp.mean(centred * centred, axis=-1, keepdims=True) + EPSILON)
    return (centred * inverse, inverse)


def norm_back(gradient, normed, inverse):
    return inverse * (
        gradient
        - jnp.mean(gradient, axis=-1, keepdims=True)
        - normed * jnp.mean(gradient * normed, axis=-1, keepdims=True)
    )


def place_kernel(count, depth, order, *refs):
    blocks, out, sems = refs[:count], refs[count], refs[count + 1]
    copies = []
    for b in range(count):
        for i in range(depth):
            at = b * depth + i
            copies.append(pltpu.make_async_copy(blocks[b].at[i], out.at[order[at]], sems.at[at]))
    for copy in copies:
        copy.start()
    for copy in copies:
        copy.wait()


def pick_kernel(count, depth, order, whole, *refs):
    blocks, sems = refs[:count], refs[count]
    copies = []
    for b in range(count):
        for i in range(depth):
            at = b * depth + i
            copies.append(pltpu.make_async_copy(whole.at[order[at]], blocks[b].at[i], sems.at[at]))
    for copy in copies:
        copy.start()
    for copy in copies:
        copy.wait()


def place(blocks, order):
    count, (depth, rows, columns) = len(blocks), blocks[0].shape
    total = count * depth
    return pl.pallas_call(
        lambda *refs: place_kernel(count, depth, *refs),
        out_shape=jax.ShapeDtypeStruct((total, rows, columns), blocks[0].dtype),
        in_specs=[pl.BlockSpec(memory_space=pltpu.SMEM)] + [pl.BlockSpec(memory_space=pl.ANY)] * count,
        out_specs=pl.BlockSpec(memory_space=pltpu.VMEM),
        scratch_shapes=[pltpu.SemaphoreType.DMA((total,))],
        compiler_params=pltpu.CompilerParams(vmem_limit_bytes=48 * 2**20),
        cost_estimate=pl.CostEstimate(
            flops=0, bytes_accessed=4 * total * rows * columns, transcendentals=0
        ),
        name="place",
    )(order, *blocks)


def pick(whole, order, count):
    total, rows, columns = whole.shape
    depth = total // count
    return pl.pallas_call(
        lambda *refs: pick_kernel(count, depth, *refs),
        out_shape=[jax.ShapeDtypeStruct((depth, rows, columns), whole.dtype)] * count,
        in_specs=[pl.BlockSpec(memory_space=pltpu.SMEM), pl.BlockSpec(memory_space=pltpu.VMEM)],
        out_specs=[pl.BlockSpec(memory_space=pl.ANY)] * count,
        scratch_shapes=[pltpu.SemaphoreType.DMA((total,))],
        compiler_params=pltpu.CompilerParams(vmem_limit_bytes=48 * 2**20),
        cost_estimate=pl.CostEstimate(
            flops=0, bytes_accessed=4 * total * rows * columns, transcendentals=0
        ),
        name="pick",
    )(order, whole)


class Grid:
    def __init__(self, seq, dp):
        self.size = {"z": 4, "y": seq // 8, "c": 2, "x": dp}
        assert seq % 8 == 0
        at, column = lax.axis_index("seq"), lax.axis_index("dp")
        sizes = self.size
        self.at = {
            "z": at // (2 * sizes["y"]),
            "y": (at // 2) % sizes["y"],
            "c": at % 2,
            "x": column,
        }

    def send(self, value, axis, shift):
        sizes = self.size
        pairs = []
        for z in range(sizes["z"]):
            for y in range(sizes["y"]):
                for c in range(2):
                    for x in range(sizes["x"]):
                        here = {"z": z, "y": y, "c": c, "x": x}
                        there = dict(here)
                        there[axis] = (here[axis] + shift) % sizes[axis]
                        pairs.append((self.flat(here), self.flat(there)))
        return lax.ppermute(value, ("seq", "dp"), pairs)

    def flat(self, p):
        sizes = self.size
        return ((p["z"] * sizes["y"] + p["y"]) * 2 + p["c"]) * sizes["x"] + p["x"]

    def swap(self, value):
        return self.send(value, "c", 1)

    def off(self, axis, shift):
        return (self.at[axis] + shift) % self.size[axis]


barrier = lax.optimization_barrier


def gather_plain(grid, piece):
    sizes = grid.size
    stack = jnp.stack([piece] + [grid.send(piece, "z", shift) for shift in range(1, sizes["z"])])
    line = [stack] + [grid.send(stack, "y", shift) for shift in range(1, sizes["y"])]
    whole = lax.all_gather(jnp.stack(line), "dp", axis=0)
    blocks = [whole[x, sy] for x in range(sizes["x"]) for sy in range(sizes["y"])]
    order = plain_order(grid, -1)
    return place(blocks, order).reshape(sizes["x"], -1, piece.shape[1])


def scatter_plain(grid, whole, rows):
    sizes = grid.size
    count = sizes["x"] * sizes["y"]
    blocks = pick(whole.reshape(-1, rows, whole.shape[-1]), plain_order(grid, 1), count)
    pairs = jnp.stack(blocks).reshape((sizes["x"], sizes["y"]) + blocks[0].shape)
    kept = lax.psum_scatter(pairs, "dp", scatter_dimension=0).astype(F32)
    total = kept[0]
    for near in range(1, sizes["y"]):
        total = total + grid.send(kept[near].astype(BF), "y", near).astype(F32)
    return scatter_z(grid, total)


def scatter_z(grid, total):
    result = total[0]
    for shift in range(1, grid.size["z"]):
        result = result + grid.send(total[shift].astype(BF), "z", shift).astype(F32)
    return result


def plain_order(grid, sign):
    sizes = grid.size
    result = []
    for x in range(sizes["x"]):
        for sy in range(sizes["y"]):
            for sz in range(sizes["z"]):
                y, z = grid.off("y", sign * sy), grid.off("z", sign * sz)
                result.append((x * sizes["z"] + z) * sizes["y"] + y)
    return jnp.stack(result).astype(jnp.int32)


def along_z(grid, piece):
    return [grid.send(piece, "z", shift) for shift in range(1, grid.size["z"])]


def to_near(grid, stack):
    return [grid.send(stack, axis, 1) for axis in "xy"]


def to_far(grid, near, cut):
    by_x, by_y = near
    return [grid.send(by_y[:, :cut], "x", 1), grid.send(by_x[:, cut:], "y", 1)]


def gathered(grid, stack, near, far, cut):
    blocks = [(stack, 0, 0, 0), (near[1], 0, 1, 0), (near[0], 1, 0, 0)]
    return Weight(grid, blocks + [(far[0], 1, 1, 0), (far[1], 1, 1, cut)])


def scatter_first(grid, blocks):
    _, away_x, _, away_y = blocks
    return [grid.send(away_x, "x", 1), grid.send(away_y, "y", 1)]


def scatter_second(grid, blocks, came):
    kept_x, _, kept_y, _ = blocks
    by_x = (kept_x[1].astype(F32) + came[0][1].astype(F32)).astype(BF)
    by_y = (kept_y[1].astype(F32) + came[1][1].astype(F32)).astype(BF)
    return [grid.send(by_x, "y", 1), grid.send(by_y, "x", 1)]


def scatter_third(blocks, came, more):
    parts = [
        kept[0].astype(F32) + near[0].astype(F32) + far.astype(F32)
        for kept, near, far in zip(blocks[::2], came, more)
    ]
    total = jnp.concatenate(parts, axis=1)
    return total[0], total[1:].astype(BF)


def scatter_last(own, came):
    for value in came:
        own = own + value.astype(F32)
    return own


def heads_of(grid, whole, rows, head_size):
    if rows % head_size == 0:
        return whole
    assert head_size == 2 * rows
    first = grid.at["c"] == 0
    halves = whole.reshape(whole.shape[0], HEADS // 2, 2, rows, -1)
    even, odd = halves[:, :, 0], halves[:, :, 1]
    kept = jnp.where(first, even, odd)
    came = grid.swap(jnp.where(first, odd, even))
    low, high = jnp.where(first, kept, came), jnp.where(first, came, kept)
    return jnp.stack([low, high], axis=2).reshape(whole.shape)


def rows_of(grid, whole, rows, head_size):
    if rows % head_size == 0:
        return whole
    first = grid.at["c"] == 0
    halves = whole.reshape(whole.shape[0], HEADS // 2, 2, rows, -1)
    low, high = halves[:, :, 0], halves[:, :, 1]
    kept = jnp.where(first, low, high)
    came = grid.swap(jnp.where(first, high, low))
    even, odd = jnp.where(first, kept, came), jnp.where(first, came, kept)
    return jnp.stack([even, odd], axis=2).reshape(whole.shape)


def split_core(grid, weight, block):
    rows, columns = weight.shape
    pairs = weight.reshape(rows, columns // (2 * block), 2, block)
    even = pairs[:, :, 0].reshape(rows, -1)
    odd = pairs[:, :, 1].reshape(rows, -1)
    first = grid.at["c"] == 0
    return (jnp.where(first, even, odd), jnp.where(first, odd, even))


def join_core(grid, own, other, block):
    rows, columns = own.shape
    first = grid.at["c"] == 0
    even = jnp.where(first, own, other).reshape(rows, -1, 1, block)
    odd = jnp.where(first, other, own).reshape(rows, -1, 1, block)
    return jnp.concatenate([even, odd], axis=2).reshape(rows, 2 * columns)


def chip_rows(grid, own, other):
    first = grid.at["c"] == 0
    return jnp.concatenate([jnp.where(first, own, other), jnp.where(first, other, own)])


def core_rows(grid, summed, block):
    rows = summed.shape[0] // 2
    first = grid.at["c"] == 0
    low, high = summed[:rows], summed[rows:]
    own = jnp.where(first, low, high)
    other = grid.swap(jnp.where(first, high, low))
    return join_core(grid, own, other, block)


GELU_A = 0.7978845608028654
GELU_B = 0.044715


def gelu(v):
    return 0.5 * v * (1.0 + jnp.tanh(GELU_A * (v + GELU_B * (v * v * v))))


def gelu_slope(v):
    inner = jnp.tanh(GELU_A * (v + GELU_B * (v * v * v)))
    return 0.5 * (1.0 + inner) + 0.5 * v * (1.0 - inner * inner) * (
        GELU_A * (1.0 + 3.0 * GELU_B * v * v)
    )


class Weight:
    def __init__(self, grid, blocks):
        self.grid = grid
        self.order = place_of(grid, -1)
        self.blocks = [block[0] for block in blocks]
        self.marks = [block[1:] for block in blocks]
        _, self.tall, wide = self.blocks[0].shape
        sizes = grid.size
        self.shape = (sizes["x"], sizes["z"] * sizes["y"] * self.tall, wide)


def place_of(grid, sign):
    sizes = grid.size
    result = []
    for axis in "xyz":
        result += [grid.off(axis, sign * shift) for shift in range(sizes[axis])]
    return jnp.stack(result).astype(jnp.int32)


def spot(whole, order, mark, sz, tall, rows):
    sx, sy, offset = mark
    x, y, z = order[sx], order[2 + sy], order[4 + sz]
    return whole.at[x, pl.ds(pl.multiple_of((z * 2 + y) * tall + offset, 16), rows), :]


def fill(blocks, order, whole, tall, marks):
    for block, mark in zip(blocks, marks):
        depth, rows, _ = block.shape

        def put(i, carry, block=block, mark=mark, rows=rows):
            spot(whole, order, mark, i, tall, rows)[...] = block[i]
            return carry

        lax.fori_loop(0, depth, put, 0)


def cost(flops, *arrays):
    return pl.CostEstimate(flops=1024, bytes_accessed=1024, transcendentals=0)


def limit(*arrays):
    total = sum(math.prod(a.shape) * jnp.dtype(a.dtype).itemsize for a in arrays)
    return pltpu.CompilerParams(vmem_limit_bytes=min(56 * 2**20, total * 9 // 8 + 16 * 2**20))


STEP = 256


def times_kernel(count, tall, marks, finish, order, rows, *refs):
    blocks, outs, whole = refs[:count], refs[count:-1], refs[-1]
    fill(blocks, order, whole, tall, marks)
    groups, total, depth = rows.shape
    for x in range(whole.shape[0]):
        for start in range(0, total, STEP):
            here = pl.ds(start, STEP)
            value = None
            for a in range(groups):
                part = jnp.dot(
                    rows[a, here, :],
                    whole[x, a * depth : (a + 1) * depth, :],
                    preferred_element_type=F32,
                )
                value = part if value is None else value + part
            finish(x, here, value, outs)


def to_group(x, here, value, outs):
    outs[0][x, here, :] = value.astype(outs[0].dtype)


def to_columns(x, here, value, outs):
    wide = value.shape[1]
    outs[0][here, x * wide : (x + 1) * wide] = value.astype(outs[0].dtype)


def to_gelu(x, here, value, outs):
    outs[0][x, here, :] = value
    outs[1][x, here, :] = gelu(value).astype(BF)


def fused(kernel, name, weight, flops, outs, before, after=()):
    blocks = weight.blocks
    whole = jax.ShapeDtypeStruct(weight.shape, BF)
    vm = pl.BlockSpec(memory_space=pltpu.VMEM)
    return pl.pallas_call(
        lambda *refs: kernel(len(blocks), weight.tall, weight.marks, *refs),
        out_shape=outs,
        in_specs=[pl.BlockSpec(memory_space=pltpu.SMEM)]
        + [vm] * (len(before) + len(blocks) + len(after)),
        out_specs=[vm] * len(outs),
        scratch_shapes=[pltpu.VMEM(weight.shape, BF)],
        compiler_params=limit(whole, whole, *before, *after, *outs),
        cost_estimate=cost(flops, whole, *before, *after, *outs),
        name=name,
    )(weight.order, *before, *blocks, *after)


def times(rows, weight, kind):
    if not isinstance(weight, Weight):
        return times_plain(rows, weight, kind)
    groups, total, depth = rows.shape
    x_count, tall, wide = weight.shape
    flops = 2 * total * tall * wide * x_count
    if kind == "gelu":
        finish = to_gelu
        outs = [
            jax.ShapeDtypeStruct((x_count, total, wide), F32),
            jax.ShapeDtypeStruct((x_count, total, wide), BF),
        ]
    elif kind == "group":
        finish, outs = to_group, [jax.ShapeDtypeStruct((x_count, total, wide), BF)]
    else:
        finish, outs = to_columns, [jax.ShapeDtypeStruct((total, x_count * wide), F32)]

    def kernel(count, tall, marks, *refs):
        times_kernel(count, tall, marks, finish, *refs)

    result = fused(kernel, "times", weight, flops, outs, (rows,))
    return result if len(result) > 1 else result[0]


def back_kernel(count, tall, marks, order, grads, *refs):
    blocks = refs[:count]
    whole, rest = refs[-1], refs[count:-1]
    out, slope = rest[-1], (rest[0] if len(rest) > 1 else None)
    fill(blocks, order, whole, tall, marks)
    x_count, depth, wide = whole.shape
    groups, total, part = out.shape
    for a in range(groups):
        for start in range(0, total, STEP):
            here = pl.ds(start, STEP)
            value = None
            for x in range(x_count):
                if len(grads.shape) == 3:
                    left = grads[x, here, :]
                else:
                    left = grads[here, x * wide : (x + 1) * wide]
                term = lax.dot_general(
                    left,
                    whole[x, a * part : (a + 1) * part, :],
                    (((1,), (1,)), ((), ())),
                    preferred_element_type=F32,
                )
                value = term if value is None else value + term
            if slope is not None:
                value = value * gelu_slope(slope[a, here, :])
            out[a, here, :] = value.astype(out.dtype)


def times_back(grads, weight, groups, kind, slope=None):
    if not isinstance(weight, Weight):
        return times_back_plain(grads, weight, groups, kind, slope)
    x_count, tall, wide = weight.shape
    total = grads.shape[-2]
    flops = 2 * total * tall * wide * x_count
    outs = [jax.ShapeDtypeStruct((groups, total, tall // groups), kind)]
    after = () if slope is None else (slope,)
    return fused(back_kernel, "times_back", weight, flops, outs, (grads,), after)[0]


def outer_kernel(tall, marks, order, rows, grads, *refs):
    blocks, whole, sems = refs[:-2], refs[-2], refs[-1]
    groups, _, depth = rows.shape
    x_count, _, wide = whole.shape
    for x in range(x_count):
        right = grads[x, :, :] if len(grads.shape) == 3 else grads[:, x * wide : (x + 1) * wide]
        for a in range(groups):
            value = lax.dot_general(
                rows[a, :, :], right, (((0,), (0,)), ((), ())), preferred_element_type=F32
            )
            whole[x, a * depth : (a + 1) * depth, :] = value.astype(BF)
    copies = []
    for block, pair in zip(blocks, marks):
        _, deep, high, _ = block.shape
        for j, mark in enumerate(pair):
            for i in range(deep):
                there = spot(whole, order, mark, i, tall, high)
                sem = sems.at[len(copies)]
                copies.append(pltpu.make_async_copy(there, block.at[j, i], sem))
    for copy in copies:
        copy.start()
    for copy in copies:
        copy.wait()


def outer(grid, rows, grads, tall, cut):
    sizes = grid.size
    groups, total, depth = rows.shape
    x_count = sizes["x"]
    wide = grads.shape[-1] if len(grads.shape) == 3 else grads.shape[1] // x_count
    outs, marks = [], []
    for start, high, by_x in ((0, cut, True), (cut, tall - cut, False)):
        for away in (0, 1):
            if high:
                outs.append(jax.ShapeDtypeStruct((2, sizes["z"], high, wide), BF))
                marks.append(
                    [(away, j, start) if by_x else (j, away, start) for j in range(2)]
                )
    assert groups * depth == sizes["z"] * sizes["y"] * tall
    whole = jax.ShapeDtypeStruct((x_count, groups * depth, wide), BF)
    vm = pl.BlockSpec(memory_space=pltpu.VMEM)
    flops = 2 * total * groups * depth * wide * x_count
    blocks = pl.pallas_call(
        lambda *refs: outer_kernel(tall, marks, *refs),
        out_shape=outs,
        in_specs=[pl.BlockSpec(memory_space=pltpu.SMEM), vm, vm],
        out_specs=[pl.BlockSpec(memory_space=pl.ANY)] * len(outs),
        scratch_shapes=[
            pltpu.VMEM(whole.shape, BF),
            pltpu.SemaphoreType.DMA((len(outs) * 2 * sizes["z"],)),
        ],
        compiler_params=limit(whole, rows, grads),
        cost_estimate=cost(flops, whole, rows, grads),
        name="outer",
    )(place_of(grid, 1), rows, grads)
    return tuple(blocks) + (None,) * (4 - len(blocks))


def head_at(number, head_size, wide):
    start = number * head_size
    return start // wide, start % wide


def soft_of(queries, keys_part, kept):
    scale = 1.0 / math.sqrt(queries.shape[1])
    scores = lax.dot_general(
        queries, keys_part, (((1,), (1,)), ((), ())), preferred_element_type=F32
    )
    scores = jnp.where(kept > 0, scores * scale, -1000000000.0)
    exponent = jnp.exp(scores - jnp.max(scores, axis=-1, keepdims=True))
    return exponent * (1.0 / jnp.sum(exponent, axis=-1, keepdims=True))


def attend_kernel(heads, head_size, padded, projected, kept, attended):
    group, length = kept.shape
    wide = projected.shape[2]

    def part(which, head, here):
        x, at = head_at(which * heads + head, head_size, wide)
        return projected[x, here, at : at + head_size]

    for g in range(group):
        here = pl.ds(g * length, length)
        mask = kept[g : g + 1, :]
        for head in range(heads):
            soft = soft_of(part(0, head, here), part(1, head, here), mask)
            value = jnp.dot(
                soft.astype(BF), part(2, head, here), preferred_element_type=F32
            ).astype(BF)
            if padded > head_size:
                value = jnp.concatenate(
                    [value, jnp.zeros((length, padded - head_size), BF)], axis=1
                )
            attended[here, head * padded : (head + 1) * padded] = value


def attend(projected, kept, padded):
    x_count, total, wide = projected.shape
    heads = HEADS // 2
    head_size = x_count * wide // (3 * heads)
    out = jax.ShapeDtypeStruct((total, heads * padded), BF)
    vm = pl.BlockSpec(memory_space=pltpu.VMEM)
    flops = 4 * total * kept.shape[1] * heads * head_size
    return pl.pallas_call(
        lambda *refs: attend_kernel(heads, head_size, padded, *refs),
        out_shape=out,
        in_specs=[vm, vm],
        out_specs=vm,
        compiler_params=limit(projected, out),
        cost_estimate=cost(8 * flops, projected, out),
        name="attend",
    )(projected, kept)


def attend_back_kernel(heads, head_size, padded, projected, kept, upstream, out):
    group, length = kept.shape
    wide = projected.shape[2]
    scale = 1.0 / math.sqrt(head_size)

    def part(which, head, here):
        x, at = head_at(which * heads + head, head_size, wide)
        return projected[x, here, at : at + head_size]

    def put(which, head, here, value):
        x, at = head_at(which * heads + head, head_size, wide)
        out[x, here, at : at + head_size] = value.astype(BF)

    for g in range(group):
        here = pl.ds(g * length, length)
        mask = kept[g : g + 1, :]
        for head in range(heads):
            queries, keys_part, values = [part(which, head, here) for which in range(3)]
            soft = soft_of(queries, keys_part, mask)
            grads = upstream[here, head * padded : head * padded + head_size]
            grad_soft = lax.dot_general(
                grads, values, (((1,), (1,)), ((), ())), preferred_element_type=F32
            )
            total = jnp.sum(soft * grad_soft, axis=-1, keepdims=True)
            grad_scores = (soft * (grad_soft - total)).astype(BF)
            first = (((0,), (0,)), ((), ()))
            put(
                0,
                head,
                here,
                jnp.dot(grad_scores, keys_part, preferred_element_type=F32) * scale,
            )
            put(
                1,
                head,
                here,
                lax.dot_general(grad_scores, queries, first, preferred_element_type=F32) * scale,
            )
            put(
                2,
                head,
                here,
                lax.dot_general(soft.astype(BF), grads, first, preferred_element_type=F32),
            )


def attend_back(projected, kept, upstream, padded):
    x_count, total, wide = projected.shape
    heads = HEADS // 2
    head_size = x_count * wide // (3 * heads)
    out = jax.ShapeDtypeStruct(projected.shape, BF)
    vm = pl.BlockSpec(memory_space=pltpu.VMEM)
    flops = 10 * total * kept.shape[1] * heads * head_size
    return pl.pallas_call(
        lambda *refs: attend_back_kernel(heads, head_size, padded, *refs),
        out_shape=out,
        in_specs=[vm, vm, vm],
        out_specs=vm,
        compiler_params=limit(projected, upstream, out),
        cost_estimate=cost(8 * flops, projected, upstream, out),
        name="attend_back",
    )(projected, kept, upstream)

def times_plain(rows, whole, kind):
    value = jnp.einsum(
        "tr,xrk->xtk",
        jnp.moveaxis(rows, 0, 1).reshape(rows.shape[1], -1),
        whole,
        preferred_element_type=F32,
    )
    if kind == "gelu":
        return value, gelu(value).astype(BF)
    if kind == "group":
        return value.astype(BF)
    return jnp.moveaxis(value, 0, 1).reshape(value.shape[1], -1)


def by_group(grads, count):
    if len(grads.shape) == 3:
        return grads
    return jnp.moveaxis(grads.reshape(grads.shape[0], count, -1), 1, 0)


def times_back_plain(grads, whole, groups, kind, slope):
    value = jnp.einsum(
        "xtk,xrk->tr", by_group(grads, whole.shape[0]), whole, preferred_element_type=F32
    )
    value = by_group(value, groups)
    if slope is not None:
        value = value * gelu_slope(slope)
    return value.astype(kind)


def outer_plain(rows, grads, count):
    flat = jnp.moveaxis(rows, 0, 1).reshape(rows.shape[1], -1)
    return jnp.einsum(
        "tr,xtk->xrk", flat, by_group(grads, count), preferred_element_type=F32
    ).astype(BF)


def exchange(value):
    return lax.all_to_all(value, ("seq", "dp"), split_axis=0, concat_axis=0, tiled=True)


def lifted_rows(seq, dp, lifted):
    latents = lifted.shape[0]
    parts = jnp.moveaxis(lifted.reshape(latents, seq, -1), 1, 0)
    every = jnp.broadcast_to(parts[:, None], (seq, dp) + parts.shape[1:])
    return exchange(every.reshape((seq * dp,) + parts.shape[1:]))


def table_sums(seq, dp, mine, modulate):
    partial = jnp.einsum("dlr,re->dle", mine, modulate, preferred_element_type=F32)
    came = exchange(partial).reshape((seq, dp) + partial.shape[1:])
    table = jnp.moveaxis(jnp.sum(came, axis=0), 0, 1)
    table = table.reshape(table.shape[0], 6, -1)
    return [table[:, number][:, None, :] for number in range(6)]


def table_gradient(seq, dp, grad_table, mine):
    latents = grad_table.shape[0]
    parts = jnp.moveaxis(grad_table.reshape(latents, dp, -1), 1, 0)
    every = jnp.broadcast_to(parts[None], (seq,) + parts.shape)
    every = exchange(every.reshape((seq * dp,) + parts.shape[1:]))
    return jnp.einsum("dlr,dle->re", mine, every, preferred_element_type=F32)


class Block:
    def __init__(self, grid, tokens, kept_tokens, grad_out):
        self.grid, self.tokens, self.grad_out = grid, tokens, grad_out
        self.shape = tokens.shape
        self.rows = tokens.shape[0] * tokens.shape[1]
        self.kept = kept_tokens.astype(F32)
        self.mask = self.kept[:, :, None]

    def share(self, value):
        flat = value.reshape(self.rows, -1)
        return jnp.concatenate([flat, self.grid.swap(flat)])

    def settle(self, value):
        return (value[: self.rows] + self.grid.swap(value[self.rows :])).reshape(self.shape)

    def begin(self, parts):
        self.parts = parts
        shift_one, scale_one, gate_one, shift_two, scale_two, gate_two = parts
        self.grad_feed = (self.mask * gate_two * self.grad_out).astype(BF)
        self.normed_one, self.inverse_one = normalize(self.tokens)
        self.hidden_one = (self.normed_one * (1.0 + scale_one) + shift_one).astype(BF)

    def after_attention(self, partial):
        _, _, gate_one, shift_two, scale_two, _ = self.parts
        self.attention_out = self.settle(partial)
        self.middle = self.tokens + self.mask * gate_one * self.attention_out
        self.normed_two, self.inverse_two = normalize(self.middle)
        self.hidden_two = (self.normed_two * (1.0 + scale_two) + shift_two).astype(BF)

    def after_feed(self, partial):
        feed = self.settle(partial)
        self.result = self.middle + self.mask * self.parts[5] * feed
        self.grad_gate_two = jnp.sum(self.mask * feed * self.grad_out, axis=1)

    def back_two(self, partial):
        _, _, gate_one, _, scale_two, _ = self.parts
        grad = self.settle(partial)
        self.grad_scale_two = jnp.sum(grad * self.normed_two, axis=1)
        self.grad_shift_two = jnp.sum(grad, axis=1)
        self.grad_middle = self.grad_out + norm_back(
            grad * (1.0 + scale_two), self.normed_two, self.inverse_two
        )
        self.grad_attention = self.share((self.mask * gate_one * self.grad_middle).astype(BF))
        self.grad_gate_one = jnp.sum(self.mask * self.attention_out * self.grad_middle, axis=1)

    def back_one(self, partial):
        grad = self.settle(partial)
        self.grad_scale_one = jnp.sum(grad * self.normed_one, axis=1)
        self.grad_shift_one = jnp.sum(grad, axis=1)
        self.grad_tokens = self.grad_middle + norm_back(
            grad * (1.0 + self.parts[1]), self.normed_one, self.inverse_one
        )

    def grad_table(self):
        parts = [
            self.grad_shift_one,
            self.grad_scale_one,
            self.grad_gate_one,
            self.grad_shift_two,
            self.grad_scale_two,
            self.grad_gate_two,
        ]
        return jnp.concatenate(parts, axis=1).astype(BF)


def rounds(grid, block, lifted, modulate, entry_piece, merge_own, expand_swap, shrink_piece):
    head_size = merge_own.shape[0]
    padded = -(-head_size // 16) * 16
    merge_piece = jnp.pad(merge_own, ((0, padded - head_size), (0, 0)))
    cut = entry_piece.shape[0] // 32 * 16 + 16
    merge_row = padded // 32 * 16 + 16
    shrink_row = shrink_piece.shape[0] // 2
    dp = grid.size["x"]
    seq = 2 * grid.size["y"] * grid.size["z"]

    block.kept_both = jnp.concatenate([block.kept, grid.swap(block.kept)])
    entry_piece, lifted, block.kept_both = barrier((entry_piece, lifted, block.kept_both))
    came = along_z(grid, entry_piece), along_z(grid, merge_piece)
    expand_piece = expand_swap()
    mine = lifted_rows(seq, dp, lifted)
    came, expand_piece, mine = barrier((came, expand_piece, mine))
    entry_stack = jnp.stack([entry_piece] + came[0])
    merge_stack = jnp.stack([merge_piece] + came[1])

    entry_near, merge_near = to_near(grid, entry_stack), to_near(grid, merge_stack)
    two = grid.send(expand_piece, "z", 2)
    block.begin(table_sums(seq, dp, mine, modulate))
    entry_near, merge_near, two, block.hidden_one, expand_piece = barrier(
        (entry_near, merge_near, two, block.hidden_one, expand_piece)
    )

    entry_far, merge_far = to_far(grid, entry_near, cut), to_far(grid, merge_near, merge_row)
    one, three = grid.send(expand_piece, "z", 1), grid.send(expand_piece, "z", 3)
    block.hidden_one = block.share(block.hidden_one)[None]
    entry_far, merge_far, one, three, block.hidden_one = barrier(
        (entry_far, merge_far, one, three, block.hidden_one)
    )
    expand_stack = jnp.stack([expand_piece, one, two, three])
    entry = gathered(grid, entry_stack, entry_near, entry_far, cut)
    merge = gathered(grid, merge_stack, merge_near, merge_far, merge_row)

    expand_near, came = to_near(grid, expand_stack), along_z(grid, shrink_piece)
    projected = times(block.hidden_one, entry, "group")
    attended = attend(projected, block.kept_both, padded)[None]
    partial = times(attended, merge, "columns")
    expand_near, came, partial = barrier((expand_near, came, partial))
    shrink_stack = jnp.stack([shrink_piece] + came)

    expand_far = to_far(grid, expand_near, cut)
    block.after_attention(partial)
    expand_far, block.hidden_two, shrink_stack = barrier(
        (expand_far, block.hidden_two, shrink_stack)
    )
    block.hidden_two = block.share(block.hidden_two)[None]

    shrink_near = to_near(grid, shrink_stack)
    expand = gathered(grid, expand_stack, expand_near, expand_far, cut)
    expanded, activated = times(block.hidden_two, expand, "gelu")
    grad_feed = block.share(block.grad_feed)
    shrink_cut = outer(grid, activated, grad_feed, shrink_piece.shape[0], shrink_row)
    shrink_near, shrink_cut, grad_feed, activated = barrier(
        (shrink_near, shrink_cut, grad_feed, activated)
    )

    shrink_far = to_far(grid, shrink_near, shrink_row)
    shrink_far, grad_feed, shrink_cut = barrier((shrink_far, grad_feed, shrink_cut))

    shrink_first = scatter_first(grid, shrink_cut)
    shrink = gathered(grid, shrink_stack, shrink_near, shrink_far, shrink_row)
    grad_expanded = times_back(grad_feed, shrink, dp, BF, expanded)
    expand_cut = outer(grid, block.hidden_two, grad_expanded, entry_piece.shape[0], cut)
    expand_cut, grad_expanded = barrier((expand_cut, grad_expanded))
    partial = times_back(grad_expanded, expand, 1, F32)[0]
    shrink_first, expand_cut, partial, activated = barrier(
        (shrink_first, expand_cut, partial, activated)
    )

    expand_first = scatter_first(grid, expand_cut)
    block.back_two(partial)
    feed = times(activated, shrink, "columns")
    expand_first, block.grad_attention, feed = barrier(
        (expand_first, block.grad_attention, feed)
    )

    shrink_second = scatter_second(grid, shrink_cut, shrink_first)
    merge_cut = outer(grid, attended, block.grad_attention, padded, merge_row)
    merge_cut, grad_attention = barrier((merge_cut, block.grad_attention))
    merge_first = scatter_first(grid, merge_cut)
    grad_attended = times_back(grad_attention, merge, 1, BF)[0]
    grad_projected = attend_back(projected, block.kept_both, grad_attended, padded)
    shrink_second, merge_first, grad_projected = barrier(
        (shrink_second, merge_first, grad_projected)
    )

    expand_second = scatter_second(grid, expand_cut, expand_first)
    shrink_sum, shrink_low = scatter_third(shrink_cut, shrink_first, shrink_second)
    shrink_z = [grid.send(shrink_low[i], "z", i + 1) for i in range(3)]
    entry_cut = outer(grid, block.hidden_one, grad_projected, entry_piece.shape[0], cut)
    partial = times_back(grad_projected, entry, 1, F32)[0]
    expand_second, shrink_z, entry_cut, partial = barrier(
        (expand_second, shrink_z, entry_cut, partial)
    )

    entry_first = scatter_first(grid, entry_cut)
    merge_second = scatter_second(grid, merge_cut, merge_first)
    expand_sum, expand_low = scatter_third(expand_cut, expand_first, expand_second)
    expand_z = [grid.send(expand_low[0], "z", 1)]
    block.after_feed(feed)
    block.back_one(partial)
    grad_table = block.grad_table()
    shrink_sum = scatter_last(shrink_sum, shrink_z)
    entry_first, merge_second, expand_z, grad_table = barrier(
        (entry_first, merge_second, expand_z, grad_table)
    )

    entry_second = scatter_second(grid, entry_cut, entry_first)
    merge_sum, merge_low = scatter_third(merge_cut, merge_first, merge_second)
    expand_z += [grid.send(expand_low[i], "z", i + 1) for i in (1, 2)]
    merge_z = [grid.send(merge_low[0], "z", 1)]
    entry_second, expand_z, merge_z, grad_table = barrier(
        (entry_second, expand_z, merge_z, grad_table)
    )

    entry_sum, entry_low = scatter_third(entry_cut, entry_first, entry_second)
    entry_z = [grid.send(entry_low[i], "z", i + 1) for i in range(3)]
    modulate_sum = table_gradient(seq, dp, grad_table, mine)
    merge_z += [grid.send(merge_low[i], "z", i + 1) for i in (1, 2)]
    expand_sum = scatter_last(expand_sum, expand_z)
    entry_z, modulate_sum = barrier((entry_z, modulate_sum))
    merge_sum = scatter_last(merge_sum, merge_z)[:head_size]
    entry_sum = scatter_last(entry_sum, entry_z)
    return entry_sum, merge_sum, expand_sum, shrink_sum, modulate_sum


def plain(grid, block, lifted, modulate, entry_piece, merge_own, expand_swap, shrink_piece):
    dp = grid.size["x"]
    head_size = block.shape[2] // HEADS
    part_rows = merge_own.shape[0]
    seq = 2 * grid.size["y"] * grid.size["z"]
    expand_piece = expand_swap()
    mine = lifted_rows(seq, dp, lifted)
    block.begin(table_sums(seq, dp, mine, modulate))
    block.hidden_one = block.share(block.hidden_one)[None]
    block.kept_both = jnp.concatenate([block.kept, grid.swap(block.kept)])
    entry = gather_plain(grid, entry_piece)
    merge = heads_of(grid, gather_plain(grid, merge_own), part_rows, head_size)
    expand = gather_plain(grid, expand_piece)
    shrink = gather_plain(grid, shrink_piece)
    projected = times(block.hidden_one, entry, "group")
    attended = attend(projected, block.kept_both, head_size)[None]
    block.after_attention(times(attended, merge, "columns"))
    block.hidden_two = block.share(block.hidden_two)[None]
    expanded, activated = times(block.hidden_two, expand, "gelu")
    block.after_feed(times(activated, shrink, "columns"))
    block.grad_feed = block.share(block.grad_feed)
    grad_shrink = outer_plain(activated, block.grad_feed, dp)
    grad_expanded = times_back(block.grad_feed, shrink, dp, BF, expanded)
    grad_expand = outer_plain(block.hidden_two, grad_expanded, dp)
    block.back_two(times_back(grad_expanded, expand, 1, F32)[0])
    grad_merge = outer_plain(attended, block.grad_attention, dp)
    grad_attended = times_back(block.grad_attention, merge, 1, BF)[0]
    grad_projected = attend_back(projected, block.kept_both, grad_attended, head_size)
    grad_entry = outer_plain(block.hidden_one, grad_projected, dp)
    block.back_one(times_back(grad_projected, entry, 1, F32)[0])
    modulate_sum = table_gradient(seq, dp, block.grad_table(), mine)
    return (
        scatter_plain(grid, grad_entry, 2 * part_rows),
        scatter_plain(grid, rows_of(grid, grad_merge, part_rows, head_size), part_rows),
        scatter_plain(grid, grad_expand, 2 * part_rows),
        scatter_plain(grid, grad_shrink, shrink_piece.shape[0]),
        modulate_sum,
    )


def local(seq, dp, *arguments):
    tokens, condition, kept_tokens, grad_out = arguments[:4]
    masters, velocities, averages = arguments[4:9], arguments[9:14], arguments[14:19]
    entry_own, merge_own, expand_own, shrink_own, modulate_own = [
        master.astype(BF) for master in masters
    ]
    grid = Grid(seq, dp)
    head_size = tokens.shape[2] // HEADS
    ff_block = shrink_own.shape[0]
    block = Block(grid, tokens, kept_tokens, grad_out)
    lifted = jax.nn.silu(condition).astype(BF)
    entry_mine, entry_theirs = split_core(grid, entry_own, head_size)
    expand_mine, expand_theirs = split_core(grid, expand_own, ff_block)
    entry_piece = chip_rows(grid, entry_mine, grid.swap(entry_theirs))

    def expand_swap():
        return chip_rows(grid, expand_mine, grid.swap(expand_theirs))

    whole_heads = merge_own.shape[0] == head_size
    act = rounds if dp == 2 and seq == HEADS and whole_heads else plain
    entry_sum, merge_sum, expand_sum, shrink_sum, modulate_sum = act(
        grid, block, lifted, modulate_own, entry_piece, merge_own, expand_swap, shrink_own
    )
    entry_sum = core_rows(grid, entry_sum, head_size)
    expand_sum = core_rows(grid, expand_sum, ff_block)
    summed = (entry_sum, merge_sum, expand_sum, shrink_sum, modulate_sum)
    result, grad_tokens = block.result, block.grad_tokens
    rows = block.rows

    rate = 0.03 / math.sqrt(rows * seq * dp)
    moved_list = []
    velocity_list = []
    average_list = []
    for master, velocity, average, gradient in zip(masters, velocities, averages, summed):
        fresh_velocity = DECAY * velocity + gradient
        moved = master - rate * (gradient + DECAY * fresh_velocity)
        moved_list.append(moved)
        velocity_list.append(fresh_velocity)
        average_list.append(0.5 * average + 0.5 * moved)
    return (result, grad_tokens) + tuple(moved_list) + tuple(velocity_list) + tuple(average_list)


def solution(mesh):
    spread = P(("seq", "dp"), None, None)
    flat = P(("seq", "dp"), None)
    weight = P("seq", "dp")
    seq, dp = mesh.shape["seq"], mesh.shape["dp"]
    return jax.shard_map(
        lambda *arguments: local(seq, dp, *arguments),
        mesh=mesh,
        in_specs=(spread, flat, flat, spread) + (weight,) * 15,
        out_specs=(spread, spread) + (weight,) * 15,
        check_vma=False,
    )
```

```python
import math

import jax
import jax.numpy as jnp
from jax import lax
from jax.experimental import pallas as pl
from jax.experimental.pallas import tpu as pltpu
from jax.sharding import PartitionSpec as P

HEADS = 16
EPSILON = 1e-06
DECAY = 0.5
BF = jnp.bfloat16
F32 = jnp.float32


def normalize(values):
    average = jnp.mean(values, axis=-1, keepdims=True)
    centred = values - average
    inverse = lax.rsqrt(jnp.mean(centred * centred, axis=-1, keepdims=True) + EPSILON)
    return (centred * inverse, inverse)


def norm_back(gradient, normed, inverse):
    return inverse * (
        gradient
        - jnp.mean(gradient, axis=-1, keepdims=True)
        - normed * jnp.mean(gradient * normed, axis=-1, keepdims=True)
    )


def place_kernel(count, depth, order, *refs):
    blocks, out, sems = refs[:count], refs[count], refs[count + 1]
    copies = []
    for b in range(count):
        for i in range(depth):
            at = b * depth + i
            copies.append(pltpu.make_async_copy(blocks[b].at[i], out.at[order[at]], sems.at[at]))
    for copy in copies:
        copy.start()
    for copy in copies:
        copy.wait()


def pick_kernel(count, depth, order, whole, *refs):
    blocks, sems = refs[:count], refs[count]
    copies = []
    for b in range(count):
        for i in range(depth):
            at = b * depth + i
            copies.append(pltpu.make_async_copy(whole.at[order[at]], blocks[b].at[i], sems.at[at]))
    for copy in copies:
        copy.start()
    for copy in copies:
        copy.wait()


def place(blocks, order):
    count, (depth, rows, columns) = len(blocks), blocks[0].shape
    total = count * depth
    return pl.pallas_call(
        lambda *refs: place_kernel(count, depth, *refs),
        out_shape=jax.ShapeDtypeStruct((total, rows, columns), blocks[0].dtype),
        in_specs=[pl.BlockSpec(memory_space=pltpu.SMEM)] + [pl.BlockSpec(memory_space=pl.ANY)] * count,
        out_specs=pl.BlockSpec(memory_space=pltpu.VMEM),
        scratch_shapes=[pltpu.SemaphoreType.DMA((total,))],
        compiler_params=pltpu.CompilerParams(vmem_limit_bytes=48 * 2**20),
        cost_estimate=pl.CostEstimate(
            flops=0, bytes_accessed=4 * total * rows * columns, transcendentals=0
        ),
        name="place",
    )(order, *blocks)


def pick(whole, order, count):
    total, rows, columns = whole.shape
    depth = total // count
    return pl.pallas_call(
        lambda *refs: pick_kernel(count, depth, *refs),
        out_shape=[jax.ShapeDtypeStruct((depth, rows, columns), whole.dtype)] * count,
        in_specs=[pl.BlockSpec(memory_space=pltpu.SMEM), pl.BlockSpec(memory_space=pltpu.VMEM)],
        out_specs=[pl.BlockSpec(memory_space=pl.ANY)] * count,
        scratch_shapes=[pltpu.SemaphoreType.DMA((total,))],
        compiler_params=pltpu.CompilerParams(vmem_limit_bytes=48 * 2**20),
        cost_estimate=pl.CostEstimate(
            flops=0, bytes_accessed=4 * total * rows * columns, transcendentals=0
        ),
        name="pick",
    )(order, whole)


class Grid:
    def __init__(self, seq, dp):
        self.size = {"z": 4, "y": seq // 8, "c": 2, "x": dp}
        assert seq % 8 == 0
        at, column = lax.axis_index("seq"), lax.axis_index("dp")
        sizes = self.size
        self.at = {
            "z": at // (2 * sizes["y"]),
            "y": (at // 2) % sizes["y"],
            "c": at % 2,
            "x": column,
        }

    def send(self, value, axis, shift):
        sizes = self.size
        pairs = []
        for z in range(sizes["z"]):
            for y in range(sizes["y"]):
                for c in range(2):
                    for x in range(sizes["x"]):
                        here = {"z": z, "y": y, "c": c, "x": x}
                        there = dict(here)
                        there[axis] = (here[axis] + shift) % sizes[axis]
                        pairs.append((self.flat(here), self.flat(there)))
        return lax.ppermute(value, ("seq", "dp"), pairs)

    def flat(self, p):
        sizes = self.size
        return ((p["z"] * sizes["y"] + p["y"]) * 2 + p["c"]) * sizes["x"] + p["x"]

    def swap(self, value):
        return self.send(value, "c", 1)

    def off(self, axis, shift):
        return (self.at[axis] + shift) % self.size[axis]


barrier = lax.optimization_barrier


def gather_plain(grid, piece):
    sizes = grid.size
    stack = jnp.stack([piece] + [grid.send(piece, "z", shift) for shift in range(1, sizes["z"])])
    line = [stack] + [grid.send(stack, "y", shift) for shift in range(1, sizes["y"])]
    whole = lax.all_gather(jnp.stack(line), "dp", axis=0)
    blocks = [whole[x, sy] for x in range(sizes["x"]) for sy in range(sizes["y"])]
    order = plain_order(grid, -1)
    return place(blocks, order).reshape(sizes["x"], -1, piece.shape[1])


def scatter_plain(grid, whole, rows):
    sizes = grid.size
    count = sizes["x"] * sizes["y"]
    blocks = pick(whole.reshape(-1, rows, whole.shape[-1]), plain_order(grid, 1), count)
    pairs = jnp.stack(blocks).reshape((sizes["x"], sizes["y"]) + blocks[0].shape)
    kept = lax.psum_scatter(pairs, "dp", scatter_dimension=0).astype(F32)
    total = kept[0]
    for near in range(1, sizes["y"]):
        total = total + grid.send(kept[near].astype(BF), "y", near).astype(F32)
    return scatter_z(grid, total)


def scatter_z(grid, total):
    result = total[0]
    for shift in range(1, grid.size["z"]):
        result = result + grid.send(total[shift].astype(BF), "z", shift).astype(F32)
    return result


def plain_order(grid, sign):
    sizes = grid.size
    result = []
    for x in range(sizes["x"]):
        for sy in range(sizes["y"]):
            for sz in range(sizes["z"]):
                y, z = grid.off("y", sign * sy), grid.off("z", sign * sz)
                result.append((x * sizes["z"] + z) * sizes["y"] + y)
    return jnp.stack(result).astype(jnp.int32)


def along_z(grid, piece):
    return [grid.send(piece, "z", shift) for shift in range(1, grid.size["z"])]


def to_near(grid, stack):
    return [grid.send(stack, axis, 1) for axis in "yx"][::-1]


def to_far(grid, near, cut):
    by_x, by_y = near
    return [grid.send(by_y[:, :cut], "x", 1), grid.send(by_x[:, cut:], "y", 1)]


def gathered(grid, stack, near, far, cut):
    blocks = [(stack, 0, 0, 0), (near[1], 0, 1, 0), (near[0], 1, 0, 0)]
    return Weight(grid, blocks + [(far[0], 1, 1, 0), (far[1], 1, 1, cut)])


def scatter_first(grid, blocks):
    _, away_x, _, away_y = blocks
    return [grid.send(away_x, "x", 1), grid.send(away_y, "y", 1)]


def scatter_second(grid, blocks, came):
    kept_x, _, kept_y, _ = blocks
    by_x = (kept_x[1].astype(F32) + came[0][1].astype(F32)).astype(BF)
    by_y = (kept_y[1].astype(F32) + came[1][1].astype(F32)).astype(BF)
    return [grid.send(by_x, "y", 1), grid.send(by_y, "x", 1)]


def scatter_third(blocks, came, more):
    def at(shift):
        parts = [
            kept[0, shift].astype(F32) + near[0, shift].astype(F32) + far[shift].astype(F32)
            for kept, near, far in zip(blocks[::2], came, more)
        ]
        return jnp.concatenate(parts)

    return at(0), [at(shift).astype(BF) for shift in range(1, blocks[0].shape[1])]


def scatter_last(own, came):
    for value in came:
        own = own + value.astype(F32)
    return own


def heads_of(grid, whole, rows, head_size):
    if rows % head_size == 0:
        return whole
    assert head_size == 2 * rows
    first = grid.at["c"] == 0
    halves = whole.reshape(whole.shape[0], HEADS // 2, 2, rows, -1)
    even, odd = halves[:, :, 0], halves[:, :, 1]
    kept = jnp.where(first, even, odd)
    came = grid.swap(jnp.where(first, odd, even))
    low, high = jnp.where(first, kept, came), jnp.where(first, came, kept)
    return jnp.stack([low, high], axis=2).reshape(whole.shape)


def rows_of(grid, whole, rows, head_size):
    if rows % head_size == 0:
        return whole
    first = grid.at["c"] == 0
    halves = whole.reshape(whole.shape[0], HEADS // 2, 2, rows, -1)
    low, high = halves[:, :, 0], halves[:, :, 1]
    kept = jnp.where(first, low, high)
    came = grid.swap(jnp.where(first, high, low))
    even, odd = jnp.where(first, kept, came), jnp.where(first, came, kept)
    return jnp.stack([even, odd], axis=2).reshape(whole.shape)


def split_core(grid, weight, block):
    rows, columns = weight.shape
    pairs = weight.reshape(rows, columns // (2 * block), 2, block)
    even = pairs[:, :, 0].reshape(rows, -1)
    odd = pairs[:, :, 1].reshape(rows, -1)
    first = grid.at["c"] == 0
    return (jnp.where(first, even, odd), jnp.where(first, odd, even))


def join_core(grid, own, other, block):
    rows, columns = own.shape
    first = grid.at["c"] == 0
    even = jnp.where(first, own, other).reshape(rows, -1, 1, block)
    odd = jnp.where(first, other, own).reshape(rows, -1, 1, block)
    return jnp.concatenate([even, odd], axis=2).reshape(rows, 2 * columns)


def chip_rows(grid, own, other):
    first = grid.at["c"] == 0
    return jnp.concatenate([jnp.where(first, own, other), jnp.where(first, other, own)])


def core_rows(grid, summed, block):
    rows = summed.shape[0] // 2
    first = grid.at["c"] == 0
    low, high = summed[:rows], summed[rows:]
    own = jnp.where(first, low, high)
    other = grid.swap(jnp.where(first, high, low))
    return join_core(grid, own, other, block)


GELU_A = 0.7978845608028654
GELU_B = 0.044715


def gelu(v):
    return 0.5 * v * (1.0 + jnp.tanh(GELU_A * (v + GELU_B * (v * v * v))))


def gelu_slope(v):
    inner = jnp.tanh(GELU_A * (v + GELU_B * (v * v * v)))
    return 0.5 * (1.0 + inner) + 0.5 * v * (1.0 - inner * inner) * (
        GELU_A * (1.0 + 3.0 * GELU_B * v * v)
    )


class Weight:
    def __init__(self, grid, blocks):
        self.grid = grid
        self.order = place_of(grid, -1)
        self.blocks = [block[0] for block in blocks]
        self.marks = [block[1:] for block in blocks]
        _, self.tall, wide = self.blocks[0].shape
        sizes = grid.size
        self.shape = (sizes["x"], sizes["z"] * sizes["y"] * self.tall, wide)


def place_of(grid, sign):
    sizes = grid.size
    result = []
    for axis in "xyz":
        result += [grid.off(axis, sign * shift) for shift in range(sizes[axis])]
    return jnp.stack(result).astype(jnp.int32)


def spot(whole, order, mark, sz, tall, rows):
    sx, sy, offset = mark
    x, y, z = order[sx], order[2 + sy], order[4 + sz]
    return whole.at[x, pl.ds(pl.multiple_of((z * 2 + y) * tall + offset, 16), rows), :]


def fill(blocks, order, whole, tall, marks):
    for block, mark in zip(blocks, marks):
        depth, rows, _ = block.shape

        def put(i, carry, block=block, mark=mark, rows=rows):
            spot(whole, order, mark, i, tall, rows)[...] = block[i]
            return carry

        lax.fori_loop(0, depth, put, 0)


def cost(flops, *arrays):
    return pl.CostEstimate(flops=1024, bytes_accessed=1024, transcendentals=0)


def limit(*arrays):
    total = sum(math.prod(a.shape) * jnp.dtype(a.dtype).itemsize for a in arrays)
    return pltpu.CompilerParams(vmem_limit_bytes=min(56 * 2**20, total * 9 // 8 + 16 * 2**20))


STEP = 256


def times_kernel(count, tall, marks, finish, order, rows, *refs):
    blocks, outs, whole = refs[:count], refs[count:-1], refs[-1]
    fill(blocks, order, whole, tall, marks)
    groups, total, depth = rows.shape
    for x in range(whole.shape[0]):
        for start in range(0, total, STEP):
            here = pl.ds(start, STEP)
            value = None
            for a in range(groups):
                part = jnp.dot(
                    rows[a, here, :],
                    whole[x, a * depth : (a + 1) * depth, :],
                    preferred_element_type=F32,
                )
                value = part if value is None else value + part
            finish(x, here, value, outs)


def to_group(x, here, value, outs):
    outs[0][x, here, :] = value.astype(outs[0].dtype)


def to_columns(x, here, value, outs):
    wide = value.shape[1]
    outs[0][here, x * wide : (x + 1) * wide] = value.astype(outs[0].dtype)


def to_gelu(x, here, value, outs):
    outs[0][x, here, :] = value
    outs[1][x, here, :] = gelu(value).astype(BF)


def fused(kernel, name, weight, flops, outs, before, after=()):
    blocks = weight.blocks
    whole = jax.ShapeDtypeStruct(weight.shape, BF)
    vm = pl.BlockSpec(memory_space=pltpu.VMEM)
    return pl.pallas_call(
        lambda *refs: kernel(len(blocks), weight.tall, weight.marks, *refs),
        out_shape=outs,
        in_specs=[pl.BlockSpec(memory_space=pltpu.SMEM)]
        + [vm] * (len(before) + len(blocks) + len(after)),
        out_specs=[vm] * len(outs),
        scratch_shapes=[pltpu.VMEM(weight.shape, BF)],
        compiler_params=limit(whole, whole, *before, *after, *outs),
        cost_estimate=cost(flops, whole, *before, *after, *outs),
        name=name,
    )(weight.order, *before, *blocks, *after)


def times(rows, weight, kind):
    if not isinstance(weight, Weight):
        return times_plain(rows, weight, kind)
    groups, total, depth = rows.shape
    x_count, tall, wide = weight.shape
    flops = 2 * total * tall * wide * x_count
    if kind == "gelu":
        finish = to_gelu
        outs = [
            jax.ShapeDtypeStruct((x_count, total, wide), F32),
            jax.ShapeDtypeStruct((x_count, total, wide), BF),
        ]
    elif kind == "group":
        finish, outs = to_group, [jax.ShapeDtypeStruct((x_count, total, wide), BF)]
    else:
        finish, outs = to_columns, [jax.ShapeDtypeStruct((total, x_count * wide), F32)]

    def kernel(count, tall, marks, *refs):
        times_kernel(count, tall, marks, finish, *refs)

    result = fused(kernel, "times", weight, flops, outs, (rows,))
    return result if len(result) > 1 else result[0]


def back_kernel(count, tall, marks, order, grads, *refs):
    blocks = refs[:count]
    whole, rest = refs[-1], refs[count:-1]
    out, slope = rest[-1], (rest[0] if len(rest) > 1 else None)
    fill(blocks, order, whole, tall, marks)
    x_count, depth, wide = whole.shape
    groups, total, part = out.shape
    for a in range(groups):
        for start in range(0, total, STEP):
            here = pl.ds(start, STEP)
            value = None
            for x in range(x_count):
                if len(grads.shape) == 3:
                    left = grads[x, here, :]
                else:
                    left = grads[here, x * wide : (x + 1) * wide]
                term = lax.dot_general(
                    left,
                    whole[x, a * part : (a + 1) * part, :],
                    (((1,), (1,)), ((), ())),
                    preferred_element_type=F32,
                )
                value = term if value is None else value + term
            if slope is not None:
                value = value * gelu_slope(slope[a, here, :])
            out[a, here, :] = value.astype(out.dtype)


def times_back(grads, weight, groups, kind, slope=None):
    if not isinstance(weight, Weight):
        return times_back_plain(grads, weight, groups, kind, slope)
    x_count, tall, wide = weight.shape
    total = grads.shape[-2]
    flops = 2 * total * tall * wide * x_count
    outs = [jax.ShapeDtypeStruct((groups, total, tall // groups), kind)]
    after = () if slope is None else (slope,)
    return fused(back_kernel, "times_back", weight, flops, outs, (grads,), after)[0]


def outer_kernel(tall, marks, order, rows, grads, *refs):
    blocks, whole, sems = refs[:-2], refs[-2], refs[-1]
    groups, _, depth = rows.shape
    x_count, _, wide = whole.shape
    for x in range(x_count):
        right = grads[x, :, :] if len(grads.shape) == 3 else grads[:, x * wide : (x + 1) * wide]
        for a in range(groups):
            value = lax.dot_general(
                rows[a, :, :], right, (((0,), (0,)), ((), ())), preferred_element_type=F32
            )
            whole[x, a * depth : (a + 1) * depth, :] = value.astype(BF)
    copies = []
    for block, pair in zip(blocks, marks):
        _, deep, high, _ = block.shape
        for j, mark in enumerate(pair):
            for i in range(deep):
                there = spot(whole, order, mark, i, tall, high)
                sem = sems.at[len(copies)]
                copies.append(pltpu.make_async_copy(there, block.at[j, i], sem))
    for copy in copies:
        copy.start()
    for copy in copies:
        copy.wait()


def outer(grid, rows, grads, tall, cut):
    sizes = grid.size
    groups, total, depth = rows.shape
    x_count = sizes["x"]
    wide = grads.shape[-1] if len(grads.shape) == 3 else grads.shape[1] // x_count
    outs, marks = [], []
    for start, high, by_x in ((0, cut, True), (cut, tall - cut, False)):
        for away in (0, 1):
            if high:
                outs.append(jax.ShapeDtypeStruct((2, sizes["z"], high, wide), BF))
                marks.append(
                    [(away, j, start) if by_x else (j, away, start) for j in range(2)]
                )
    assert groups * depth == sizes["z"] * sizes["y"] * tall
    whole = jax.ShapeDtypeStruct((x_count, groups * depth, wide), BF)
    vm = pl.BlockSpec(memory_space=pltpu.VMEM)
    flops = 2 * total * groups * depth * wide * x_count
    blocks = pl.pallas_call(
        lambda *refs: outer_kernel(tall, marks, *refs),
        out_shape=outs,
        in_specs=[pl.BlockSpec(memory_space=pltpu.SMEM), vm, vm],
        out_specs=[pl.BlockSpec(memory_space=pl.ANY)] * len(outs),
        scratch_shapes=[
            pltpu.VMEM(whole.shape, BF),
            pltpu.SemaphoreType.DMA((len(outs) * 2 * sizes["z"],)),
        ],
        compiler_params=limit(whole, rows, grads),
        cost_estimate=cost(flops, whole, rows, grads),
        name="outer",
    )(place_of(grid, 1), rows, grads)
    return tuple(blocks) + (None,) * (4 - len(blocks))


def head_at(number, head_size, wide):
    start = number * head_size
    return start // wide, start % wide


def soft_of(queries, keys_part, kept):
    scale = 1.0 / math.sqrt(queries.shape[1])
    scores = lax.dot_general(
        queries, keys_part, (((1,), (1,)), ((), ())), preferred_element_type=F32
    )
    scores = jnp.where(kept > 0, scores * scale, -1000000000.0)
    exponent = jnp.exp(scores - jnp.max(scores, axis=-1, keepdims=True))
    return exponent * (1.0 / jnp.sum(exponent, axis=-1, keepdims=True))


def attend_kernel(heads, head_size, padded, projected, kept, attended):
    group, length = kept.shape
    wide = projected.shape[2]

    def part(which, head, here):
        x, at = head_at(which * heads + head, head_size, wide)
        return projected[x, here, at : at + head_size]

    for g in range(group):
        here = pl.ds(g * length, length)
        mask = kept[g : g + 1, :]
        for head in range(heads):
            soft = soft_of(part(0, head, here), part(1, head, here), mask)
            value = jnp.dot(
                soft.astype(BF), part(2, head, here), preferred_element_type=F32
            ).astype(BF)
            if padded > head_size:
                value = jnp.concatenate(
                    [value, jnp.zeros((length, padded - head_size), BF)], axis=1
                )
            attended[here, head * padded : (head + 1) * padded] = value


def attend(projected, kept, padded):
    x_count, total, wide = projected.shape
    heads = HEADS // 2
    head_size = x_count * wide // (3 * heads)
    out = jax.ShapeDtypeStruct((total, heads * padded), BF)
    vm = pl.BlockSpec(memory_space=pltpu.VMEM)
    flops = 4 * total * kept.shape[1] * heads * head_size
    return pl.pallas_call(
        lambda *refs: attend_kernel(heads, head_size, padded, *refs),
        out_shape=out,
        in_specs=[vm, vm],
        out_specs=vm,
        compiler_params=limit(projected, out),
        cost_estimate=cost(8 * flops, projected, out),
        name="attend",
    )(projected, kept)


def attend_back_kernel(heads, head_size, padded, projected, kept, upstream, out):
    group, length = kept.shape
    wide = projected.shape[2]
    scale = 1.0 / math.sqrt(head_size)

    def part(which, head, here):
        x, at = head_at(which * heads + head, head_size, wide)
        return projected[x, here, at : at + head_size]

    def put(which, head, here, value):
        x, at = head_at(which * heads + head, head_size, wide)
        out[x, here, at : at + head_size] = value.astype(BF)

    for g in range(group):
        here = pl.ds(g * length, length)
        mask = kept[g : g + 1, :]
        for head in range(heads):
            queries, keys_part, values = [part(which, head, here) for which in range(3)]
            soft = soft_of(queries, keys_part, mask)
            grads = upstream[here, head * padded : head * padded + head_size]
            grad_soft = lax.dot_general(
                grads, values, (((1,), (1,)), ((), ())), preferred_element_type=F32
            )
            total = jnp.sum(soft * grad_soft, axis=-1, keepdims=True)
            grad_scores = (soft * (grad_soft - total)).astype(BF)
            first = (((0,), (0,)), ((), ()))
            put(
                0,
                head,
                here,
                jnp.dot(grad_scores, keys_part, preferred_element_type=F32) * scale,
            )
            put(
                1,
                head,
                here,
                lax.dot_general(grad_scores, queries, first, preferred_element_type=F32) * scale,
            )
            put(
                2,
                head,
                here,
                lax.dot_general(soft.astype(BF), grads, first, preferred_element_type=F32),
            )


def attend_back(projected, kept, upstream, padded):
    x_count, total, wide = projected.shape
    heads = HEADS // 2
    head_size = x_count * wide // (3 * heads)
    out = jax.ShapeDtypeStruct(projected.shape, BF)
    vm = pl.BlockSpec(memory_space=pltpu.VMEM)
    flops = 10 * total * kept.shape[1] * heads * head_size
    return pl.pallas_call(
        lambda *refs: attend_back_kernel(heads, head_size, padded, *refs),
        out_shape=out,
        in_specs=[vm, vm, vm],
        out_specs=vm,
        compiler_params=limit(projected, upstream, out),
        cost_estimate=cost(8 * flops, projected, upstream, out),
        name="attend_back",
    )(projected, kept, upstream)

def times_plain(rows, whole, kind):
    value = jnp.einsum(
        "tr,xrk->xtk",
        jnp.moveaxis(rows, 0, 1).reshape(rows.shape[1], -1),
        whole,
        preferred_element_type=F32,
    )
    if kind == "gelu":
        return value, gelu(value).astype(BF)
    if kind == "group":
        return value.astype(BF)
    return jnp.moveaxis(value, 0, 1).reshape(value.shape[1], -1)


def by_group(grads, count):
    if len(grads.shape) == 3:
        return grads
    return jnp.moveaxis(grads.reshape(grads.shape[0], count, -1), 1, 0)


def times_back_plain(grads, whole, groups, kind, slope):
    value = jnp.einsum(
        "xtk,xrk->tr", by_group(grads, whole.shape[0]), whole, preferred_element_type=F32
    )
    value = by_group(value, groups)
    if slope is not None:
        value = value * gelu_slope(slope)
    return value.astype(kind)


def outer_plain(rows, grads, count):
    flat = jnp.moveaxis(rows, 0, 1).reshape(rows.shape[1], -1)
    return jnp.einsum(
        "tr,xtk->xrk", flat, by_group(grads, count), preferred_element_type=F32
    ).astype(BF)


def exchange(value):
    return lax.all_to_all(value, ("seq", "dp"), split_axis=0, concat_axis=0, tiled=True)


def lifted_rows(seq, dp, lifted):
    latents = lifted.shape[0]
    parts = jnp.moveaxis(lifted.reshape(latents, seq, -1), 1, 0)
    every = jnp.broadcast_to(parts[:, None], (seq, dp) + parts.shape[1:])
    return exchange(every.reshape((seq * dp,) + parts.shape[1:]))


def table_sums(seq, dp, mine, modulate):
    partial = jnp.einsum("dlr,re->dle", mine, modulate, preferred_element_type=F32)
    came = exchange(partial).reshape((seq, dp) + partial.shape[1:])
    table = jnp.moveaxis(jnp.sum(came, axis=0), 0, 1)
    table = table.reshape(table.shape[0], 6, -1)
    return [table[:, number][:, None, :] for number in range(6)]


def table_gradient(seq, dp, grad_table, mine):
    latents = grad_table.shape[0]
    parts = jnp.moveaxis(grad_table.reshape(latents, dp, -1), 1, 0)
    every = jnp.broadcast_to(parts[None], (seq,) + parts.shape)
    every = exchange(every.reshape((seq * dp,) + parts.shape[1:]))
    return jnp.einsum("dlr,dle->re", mine, every, preferred_element_type=F32)


class Block:
    def __init__(self, grid, tokens, kept_tokens, grad_out):
        self.grid, self.tokens, self.grad_out = grid, tokens, grad_out
        self.shape = tokens.shape
        self.rows = tokens.shape[0] * tokens.shape[1]
        self.kept = kept_tokens.astype(F32)
        self.mask = self.kept[:, :, None]

    def share(self, value):
        flat = value.reshape(self.rows, -1)
        return jnp.concatenate([flat, self.grid.swap(flat)])

    def settle(self, value):
        return (value[: self.rows] + self.grid.swap(value[self.rows :])).reshape(self.shape)

    def begin(self, parts):
        self.parts = parts
        shift_one, scale_one, gate_one, shift_two, scale_two, gate_two = parts
        self.grad_feed = (self.mask * gate_two * self.grad_out).astype(BF)
        self.normed_one, self.inverse_one = normalize(self.tokens)
        self.hidden_one = (self.normed_one * (1.0 + scale_one) + shift_one).astype(BF)

    def after_attention(self, partial):
        _, _, gate_one, shift_two, scale_two, _ = self.parts
        self.attention_out = self.settle(partial)
        self.middle = self.tokens + self.mask * gate_one * self.attention_out
        self.normed_two, self.inverse_two = normalize(self.middle)
        self.hidden_two = (self.normed_two * (1.0 + scale_two) + shift_two).astype(BF)

    def after_feed(self, partial):
        feed = self.settle(partial)
        self.result = self.middle + self.mask * self.parts[5] * feed
        self.grad_gate_two = jnp.sum(self.mask * feed * self.grad_out, axis=1)

    def back_two(self, partial):
        _, _, gate_one, _, scale_two, _ = self.parts
        grad = self.settle(partial)
        self.grad_scale_two = jnp.sum(grad * self.normed_two, axis=1)
        self.grad_shift_two = jnp.sum(grad, axis=1)
        self.grad_middle = self.grad_out + norm_back(
            grad * (1.0 + scale_two), self.normed_two, self.inverse_two
        )
        self.grad_attention = self.share((self.mask * gate_one * self.grad_middle).astype(BF))
        self.grad_gate_one = jnp.sum(self.mask * self.attention_out * self.grad_middle, axis=1)

    def back_one(self, partial):
        grad = self.settle(partial)
        self.grad_scale_one = jnp.sum(grad * self.normed_one, axis=1)
        self.grad_shift_one = jnp.sum(grad, axis=1)
        self.grad_tokens = self.grad_middle + norm_back(
            grad * (1.0 + self.parts[1]), self.normed_one, self.inverse_one
        )

    def grad_table(self):
        parts = [
            self.grad_shift_one,
            self.grad_scale_one,
            self.grad_gate_one,
            self.grad_shift_two,
            self.grad_scale_two,
            self.grad_gate_two,
        ]
        return jnp.concatenate(parts, axis=1).astype(BF)


def rounds(grid, block, lifted, modulate, entry_piece, merge_own, expand_swap, shrink_piece):
    head_size = merge_own.shape[0]
    padded = -(-head_size // 16) * 16
    merge_piece = jnp.pad(merge_own, ((0, padded - head_size), (0, 0)))
    cut = entry_piece.shape[0] // 32 * 16 + 16
    merge_row = padded // 32 * 16 + 16
    shrink_row = shrink_piece.shape[0] // 2
    dp = grid.size["x"]
    seq = 2 * grid.size["y"] * grid.size["z"]

    block.kept_both = jnp.concatenate([block.kept, grid.swap(block.kept)])
    entry_piece, lifted, block.kept_both = barrier((entry_piece, lifted, block.kept_both))
    came = along_z(grid, entry_piece), along_z(grid, merge_piece)
    expand_piece = expand_swap()
    mine = lifted_rows(seq, dp, lifted)
    came, expand_piece, mine = barrier((came, expand_piece, mine))
    entry_stack = jnp.stack([entry_piece] + came[0])
    merge_stack = jnp.stack([merge_piece] + came[1])

    entry_near, merge_near = to_near(grid, entry_stack), to_near(grid, merge_stack)
    two = grid.send(expand_piece, "z", 2)
    block.begin(table_sums(seq, dp, mine, modulate))
    entry_near, merge_near, two, block.hidden_one, expand_piece = barrier(
        (entry_near, merge_near, two, block.hidden_one, expand_piece)
    )

    entry_far, merge_far = to_far(grid, entry_near, cut), to_far(grid, merge_near, merge_row)
    one, three = grid.send(expand_piece, "z", 1), grid.send(expand_piece, "z", 3)
    block.hidden_one = block.share(block.hidden_one)[None]
    entry_far, merge_far, one, three, block.hidden_one = barrier(
        (entry_far, merge_far, one, three, block.hidden_one)
    )
    expand_stack = jnp.stack([expand_piece, one, two, three])
    entry = gathered(grid, entry_stack, entry_near, entry_far, cut)
    merge = gathered(grid, merge_stack, merge_near, merge_far, merge_row)

    expand_near, came = to_near(grid, expand_stack), along_z(grid, shrink_piece)
    projected = times(block.hidden_one, entry, "group")
    attended = attend(projected, block.kept_both, padded)[None]
    partial = times(attended, merge, "columns")
    expand_near, came, partial = barrier((expand_near, came, partial))
    shrink_stack = jnp.stack([shrink_piece] + came)

    expand_far = to_far(grid, expand_near, cut)
    block.after_attention(partial)
    expand_far, block.hidden_two, shrink_stack = barrier(
        (expand_far, block.hidden_two, shrink_stack)
    )
    block.hidden_two = block.share(block.hidden_two)[None]

    shrink_near = to_near(grid, shrink_stack)
    expand = gathered(grid, expand_stack, expand_near, expand_far, cut)
    expanded, activated = times(block.hidden_two, expand, "gelu")
    grad_feed = block.share(block.grad_feed)
    shrink_cut = outer(grid, activated, grad_feed, shrink_piece.shape[0], shrink_row)
    shrink_near, shrink_cut, grad_feed, activated = barrier(
        (shrink_near, shrink_cut, grad_feed, activated)
    )

    shrink_far = to_far(grid, shrink_near, shrink_row)
    shrink_far, grad_feed, shrink_cut = barrier((shrink_far, grad_feed, shrink_cut))

    shrink_first = scatter_first(grid, shrink_cut)
    shrink = gathered(grid, shrink_stack, shrink_near, shrink_far, shrink_row)
    grad_expanded = times_back(grad_feed, shrink, dp, BF, expanded)
    expand_cut = outer(grid, block.hidden_two, grad_expanded, entry_piece.shape[0], cut)
    expand_cut, grad_expanded = barrier((expand_cut, grad_expanded))
    partial = times_back(grad_expanded, expand, 1, F32)[0]
    shrink_first, expand_cut, partial, activated = barrier(
        (shrink_first, expand_cut, partial, activated)
    )

    expand_first = scatter_first(grid, expand_cut)
    block.back_two(partial)
    feed = times(activated, shrink, "columns")
    expand_first, block.grad_attention, feed = barrier(
        (expand_first, block.grad_attention, feed)
    )

    shrink_second = scatter_second(grid, shrink_cut, shrink_first)
    merge_cut = outer(grid, attended, block.grad_attention, padded, merge_row)
    merge_cut, grad_attention = barrier((merge_cut, block.grad_attention))
    merge_first = scatter_first(grid, merge_cut)
    grad_attended = times_back(grad_attention, merge, 1, BF)[0]
    grad_projected = attend_back(projected, block.kept_both, grad_attended, padded)
    shrink_second, merge_first, grad_projected = barrier(
        (shrink_second, merge_first, grad_projected)
    )

    expand_second = scatter_second(grid, expand_cut, expand_first)
    shrink_sum, shrink_low = scatter_third(shrink_cut, shrink_first, shrink_second)
    shrink_z = [grid.send(shrink_low[i], "z", i + 1) for i in range(3)]
    entry_cut = outer(grid, block.hidden_one, grad_projected, entry_piece.shape[0], cut)
    partial = times_back(grad_projected, entry, 1, F32)[0]
    expand_second, shrink_z, entry_cut, partial = barrier(
        (expand_second, shrink_z, entry_cut, partial)
    )

    entry_first = scatter_first(grid, entry_cut)
    merge_second = scatter_second(grid, merge_cut, merge_first)
    expand_sum, expand_low = scatter_third(expand_cut, expand_first, expand_second)
    expand_z = [grid.send(expand_low[1], "z", 2)]
    block.after_feed(feed)
    block.back_one(partial)
    grad_table = block.grad_table()
    shrink_sum = scatter_last(shrink_sum, shrink_z)
    entry_first, merge_second, expand_z, grad_table = barrier(
        (entry_first, merge_second, expand_z, grad_table)
    )

    entry_second = scatter_second(grid, entry_cut, entry_first)
    merge_sum, merge_low = scatter_third(merge_cut, merge_first, merge_second)
    expand_z += [grid.send(expand_low[i], "z", i + 1) for i in (0, 2)]
    merge_z = [grid.send(merge_low[0], "z", 1)]
    entry_second, expand_z, merge_z, grad_table = barrier(
        (entry_second, expand_z, merge_z, grad_table)
    )

    entry_sum, entry_low = scatter_third(entry_cut, entry_first, entry_second)
    entry_z = [grid.send(entry_low[i], "z", i + 1) for i in range(3)]
    modulate_sum = table_gradient(seq, dp, grad_table, mine)
    merge_z += [grid.send(merge_low[i], "z", i + 1) for i in (1, 2)]
    expand_sum = scatter_last(expand_sum, expand_z)
    entry_z, modulate_sum = barrier((entry_z, modulate_sum))
    merge_sum = scatter_last(merge_sum, merge_z)[:head_size]
    entry_sum = scatter_last(entry_sum, entry_z)
    return entry_sum, merge_sum, expand_sum, shrink_sum, modulate_sum


def plain(grid, block, lifted, modulate, entry_piece, merge_own, expand_swap, shrink_piece):
    dp = grid.size["x"]
    head_size = block.shape[2] // HEADS
    part_rows = merge_own.shape[0]
    seq = 2 * grid.size["y"] * grid.size["z"]
    expand_piece = expand_swap()
    mine = lifted_rows(seq, dp, lifted)
    block.begin(table_sums(seq, dp, mine, modulate))
    block.hidden_one = block.share(block.hidden_one)[None]
    block.kept_both = jnp.concatenate([block.kept, grid.swap(block.kept)])
    entry = gather_plain(grid, entry_piece)
    merge = heads_of(grid, gather_plain(grid, merge_own), part_rows, head_size)
    expand = gather_plain(grid, expand_piece)
    shrink = gather_plain(grid, shrink_piece)
    projected = times(block.hidden_one, entry, "group")
    attended = attend(projected, block.kept_both, head_size)[None]
    block.after_attention(times(attended, merge, "columns"))
    block.hidden_two = block.share(block.hidden_two)[None]
    expanded, activated = times(block.hidden_two, expand, "gelu")
    block.after_feed(times(activated, shrink, "columns"))
    block.grad_feed = block.share(block.grad_feed)
    grad_shrink = outer_plain(activated, block.grad_feed, dp)
    grad_expanded = times_back(block.grad_feed, shrink, dp, BF, expanded)
    grad_expand = outer_plain(block.hidden_two, grad_expanded, dp)
    block.back_two(times_back(grad_expanded, expand, 1, F32)[0])
    grad_merge = outer_plain(attended, block.grad_attention, dp)
    grad_attended = times_back(block.grad_attention, merge, 1, BF)[0]
    grad_projected = attend_back(projected, block.kept_both, grad_attended, head_size)
    grad_entry = outer_plain(block.hidden_one, grad_projected, dp)
    block.back_one(times_back(grad_projected, entry, 1, F32)[0])
    modulate_sum = table_gradient(seq, dp, block.grad_table(), mine)
    return (
        scatter_plain(grid, grad_entry, 2 * part_rows),
        scatter_plain(grid, rows_of(grid, grad_merge, part_rows, head_size), part_rows),
        scatter_plain(grid, grad_expand, 2 * part_rows),
        scatter_plain(grid, grad_shrink, shrink_piece.shape[0]),
        modulate_sum,
    )


def local(seq, dp, *arguments):
    tokens, condition, kept_tokens, grad_out = arguments[:4]
    masters, velocities, averages = arguments[4:9], arguments[9:14], arguments[14:19]
    entry_own, merge_own, expand_own, shrink_own, modulate_own = [
        master.astype(BF) for master in masters
    ]
    grid = Grid(seq, dp)
    head_size = tokens.shape[2] // HEADS
    ff_block = shrink_own.shape[0]
    block = Block(grid, tokens, kept_tokens, grad_out)
    lifted = jax.nn.silu(condition).astype(BF)
    entry_mine, entry_theirs = split_core(grid, entry_own, head_size)
    expand_mine, expand_theirs = split_core(grid, expand_own, ff_block)
    entry_piece = chip_rows(grid, entry_mine, grid.swap(entry_theirs))

    def expand_swap():
        return chip_rows(grid, expand_mine, grid.swap(expand_theirs))

    whole_heads = merge_own.shape[0] == head_size
    act = rounds if dp == 2 and seq == HEADS and whole_heads else plain
    entry_sum, merge_sum, expand_sum, shrink_sum, modulate_sum = act(
        grid, block, lifted, modulate_own, entry_piece, merge_own, expand_swap, shrink_own
    )
    entry_sum = core_rows(grid, entry_sum, head_size)
    expand_sum = core_rows(grid, expand_sum, ff_block)
    summed = (entry_sum, merge_sum, expand_sum, shrink_sum, modulate_sum)
    result, grad_tokens = block.result, block.grad_tokens
    rows = block.rows

    rate = 0.03 / math.sqrt(rows * seq * dp)
    moved_list = []
    velocity_list = []
    average_list = []
    for master, velocity, average, gradient in zip(masters, velocities, averages, summed):
        fresh_velocity = DECAY * velocity + gradient
        moved = master - rate * (gradient + DECAY * fresh_velocity)
        moved_list.append(moved)
        velocity_list.append(fresh_velocity)
        average_list.append(0.5 * average + 0.5 * moved)
    return (result, grad_tokens) + tuple(moved_list) + tuple(velocity_list) + tuple(average_list)


def solution(mesh):
    spread = P(("seq", "dp"), None, None)
    flat = P(("seq", "dp"), None)
    weight = P("seq", "dp")
    seq, dp = mesh.shape["seq"], mesh.shape["dp"]
    return jax.shard_map(
        lambda *arguments: local(seq, dp, *arguments),
        mesh=mesh,
        in_specs=(spread, flat, flat, spread) + (weight,) * 15,
        out_specs=(spread, spread) + (weight,) * 15,
        check_vma=False,
    )
```
